32 devices in a mesh: row: 4 (over z), col: 8 (over y, x, core).
Axes of the slice: x: 2, y: 2, z: 4, core: 2. Of those that a mesh axis runs over, the one named last changes fastest.
Arguments:
- photo_features: bfloat16 [384, 1152], P(('row', 'col')), may hold values from -6 to 6
- sentence_features: bfloat16 [384, 1152], P(('row', 'col')), may hold values from -6 to 6
- described_photo_number: int32 [384], P(('row', 'col')), may hold values from 0 to 383, each once
- logit_multiplier: float32 [], replicated, may hold values from 3 to 8
- logit_offset: float32 [], replicated, may hold values from -4 to -1
Outputs:
- img_grad: float32 [384, 1152], P(('row', 'col'))
- txt_grad: float32 [384, 1152], P(('row', 'col'))
The draws below stay inside these ranges and needn't reach their ends.
Inputs may be any that keep to these rules, and one draw needn't show every extreme that they name: `described_photo_number`: every image index appears exactly once among the text ids.
All inputs are finite; a program needn't handle non-finite values.
Results may differ from the reference program's by a relative error of at most 0.004.
Values may be sent and summed in bfloat16 or wider, within the bound.
A program may use at most 64 MiB of HBM per device.

```python
import jax
import jax.numpy as jnp
from jax import lax

D = 1152
PAIRS = 384
N_ROW = 4


def level_of(key, extent, split, low, top_value):
    gain = 1.0
    for dim, shards_of in split:
        steps = jax.random.uniform(jax.random.fold_in(jax.random.fold_in(key, 6), dim), (shards_of,), jnp.float32, low / len(split), top_value / len(split))
        gain = gain * jnp.repeat(jnp.exp(steps), extent[dim] // shards_of).reshape((-1,) + (1,) * (len(extent) - 1 - dim))
    return gain


def centred(key, extent, deviation, most, split=(), held_as=jnp.bfloat16):
    drawn = deviation * jax.random.normal(key, extent, jnp.float32)
    if split:
        drawn = drawn * level_of(key, extent, split, -0.22, 0.18)
    return jnp.clip(drawn, -most, most).astype(held_as)


def setup_inputs(seed: int = 0) -> dict:
    key_list = jax.random.split(jax.random.key(seed), 6)
    photo_features = centred(key_list[0], (PAIRS, D), 1.0, 6.0, ((0, 32),))
    sentence_features = centred(key_list[1], (PAIRS, D), 1.0, 6.0, ((0, 32),))
    described_photo_number = jax.random.permutation(key_list[2], PAIRS).astype(jnp.int32)
    logit_multiplier = jnp.clip(jax.random.uniform(key_list[3], (), jnp.float32, 3.0, 8.0), 3.0, 8.0)
    logit_offset = jnp.clip(jax.random.uniform(key_list[4], (), jnp.float32, -4.0, -1.0), -4.0, -1.0)
    return dict(photo_features=photo_features, sentence_features=sentence_features, described_photo_number=described_photo_number, logit_multiplier=logit_multiplier, logit_offset=logit_offset)


def unit_rows(raw):
    values = raw.astype(jnp.float32)
    scale = lax.rsqrt(lax.optimization_barrier(jnp.sum(values * values, axis=1, keepdims=True)) + 1e-06)
    return (values * scale, scale)

def back_through(unit, scale, upstream):
    inner = lax.optimization_barrier(jnp.sum(unit * upstream, axis=1, keepdims=True))
    return scale * (upstream - unit * inner)

def reference(photo_features, sentence_features, described_photo_number, logit_multiplier, logit_offset):
    img_unit, img_scale = unit_rows(photo_features)
    txt_unit, txt_scale = unit_rows(sentence_features)
    img_send = img_unit.astype(jnp.bfloat16)
    sentence_sent_onward = txt_unit.astype(jnp.bfloat16)
    block_rows = PAIRS // N_ROW

    def one_block(txt_acc, index):
        start = (index * block_rows).astype(jnp.int32)
        photo_entries = lax.dynamic_slice_in_dim(img_send, start, block_rows, 0)
        similarity_logits = logit_multiplier * jnp.dot(photo_entries, sentence_sent_onward.T, preferred_element_type=jnp.float32) + logit_offset
        ids = start + lax.iota(jnp.int32, block_rows)
        match_polarity = jnp.where(ids[:, None] == described_photo_number[None, :], 1.0, -1.0).astype(similarity_logits.dtype)
        coefficient_table = (logit_multiplier * -match_polarity * jax.nn.sigmoid(-match_polarity * similarity_logits)).astype(jnp.bfloat16)
        img_up = jnp.dot(coefficient_table, sentence_sent_onward, preferred_element_type=jnp.float32)
        txt_acc = txt_acc + jnp.dot(coefficient_table.T, photo_entries, preferred_element_type=jnp.float32)
        return (txt_acc, img_up)
    start_acc = jnp.zeros((PAIRS, D), jnp.float32)
    txt_upstream, img_parts = lax.scan(one_block, start_acc, jnp.arange(N_ROW, dtype=jnp.int32))
    img_upstream = img_parts.reshape(PAIRS, D)
    return (back_through(img_unit, img_scale, img_upstream), back_through(txt_unit, txt_scale, txt_upstream))
```

```python
import functools

import jax
import jax.numpy as jnp
from jax import lax
from jax.experimental import pallas as pl
from jax.experimental.pallas import tpu as pltpu
from jax.sharding import PartitionSpec as P

MESH = pl.DeviceIdType.MESH
TILE = 16
F32 = jnp.float32
BF16 = jnp.bfloat16


def partner(me, step, count):
    if count & (count - 1):
        return lax.rem(me + step, count), lax.rem(me + count - step, count)
    bit = 1
    peer = me
    while bit <= step:
        if step & bit:
            peer = peer + bit * (1 - 2 * lax.rem(me // bit, 2))
        bit *= 2
    return peer, peer


def unit_rows(values):
    scale = lax.rsqrt(jnp.sum(values * values, axis=1, keepdims=True) + 1e-06)
    return values * scale, scale


def back_through(unit, scale, upstream):
    inner = jnp.sum(unit * upstream, axis=1, keepdims=True)
    return scale * (upstream - unit * inner)


def kernel(
    n_row, n_col, own, pad,
    ids_ref, mul_ref, off_ref, img_hbm, txt_hbm, img_grad, txt_grad,
    img_raw, txt_raw, img_unit, txt_unit, img_all, txt_all, img_part, txt_part, img_in, txt_in,
    load_sem, img_send, img_recv, txt_send, txt_recv, img_back, img_got, txt_back, txt_got,
):
    row, col = lax.axis_index("row"), lax.axis_index("col")
    loads = [
        pltpu.make_async_copy(img_hbm, img_raw, load_sem.at[0]),
        pltpu.make_async_copy(txt_hbm, txt_raw, load_sem.at[1]),
    ]
    for load in loads:
        load.start()

    col_peer = [None] + [partner(col, d, n_col) for d in range(1, n_col)]
    row_peer = [None] + [partner(row, d, n_row) for d in range(1, n_row)]
    barrier = pltpu.get_barrier_semaphore()
    for d in range(1, n_col):
        pl.semaphore_signal(barrier, inc=1, device_id=(row, col_peer[d][1]), device_id_type=MESH)
    for d in range(1, n_row):
        pl.semaphore_signal(barrier, inc=1, device_id=(row_peer[d][1], col), device_id_type=MESH)

    width = img_raw.shape[1]
    lanes = n_row * pad
    lane = lax.rem(lax.broadcasted_iota(jnp.int32, (1, width), 1), pad)
    numbers = jnp.zeros((1, width), jnp.int32)
    for t in range(own):
        numbers = jnp.where(lane == t, ids_ref[t], numbers)
    low = lax.rem(numbers, 256).astype(F32)
    high = (numbers // 256).astype(F32)

    loads[1].wait()
    txt_value, txt_scale = unit_rows(txt_raw[...].astype(F32))
    txt_unit[pl.ds(0, own)] = txt_value
    txt_unit[pl.ds(own, 1)] = low
    txt_unit[pl.ds(own + 1, 1)] = high
    txt_unit[pl.ds(own + 2, pad - own - 2)] = jnp.zeros((pad - own - 2, width), F32)
    txt_all[pl.ds(0, pad)] = txt_unit[...].astype(BF16)
    loads[0].wait()
    img_value, img_scale = unit_rows(img_raw[...].astype(F32))
    img_unit[pl.ds(0, own)] = img_value
    img_unit[pl.ds(own, pad - own)] = jnp.zeros((pad - own, width), F32)
    img_all[pl.ds(0, pad)] = img_unit[...].astype(BF16)

    pl.semaphore_wait(barrier, n_col + n_row - 2)

    def send(src, dst, d, sems, peer):
        return pltpu.make_async_remote_copy(
            src_ref=src, dst_ref=dst.at[pl.ds(d * pad, pad)],
            send_sem=sems[0].at[d], recv_sem=sems[1].at[d],
            device_id=peer, device_id_type=MESH,
        )

    txt_copies = [
        send(txt_all.at[pl.ds(0, pad)], txt_all, d, (txt_send, txt_recv), (row_peer[d][0], col))
        for d in range(1, n_row)
    ]
    img_copies = [
        send(img_all.at[pl.ds(0, pad)], img_all, d, (img_send, img_recv), (row, col_peer[d][0]))
        for d in range(1, n_col)
    ]
    for copy in reversed(txt_copies):
        copy.start()
    for copy in reversed(img_copies):
        copy.start()

    multiplier, offset = mul_ref[0], off_ref[0]
    place = lax.broadcasted_iota(jnp.int32, (n_col * pad, 1), 0)
    slot, entry = place // pad, lax.rem(place, pad)
    owner = jnp.zeros((n_col * pad, 1), jnp.int32) + col
    for d in range(1, n_col):
        owner = jnp.where(slot == d, col_peer[d][1], owner)
    img_ids = (row * n_col + owner) * own + entry
    at = lax.broadcasted_iota(jnp.int32, (1, lanes), 1)

    for copy in txt_copies:
        copy.wait_recv()
    digits = []
    for digit in range(2):
        line = jnp.zeros((1, lanes), F32)
        for d in range(n_row):
            block = txt_all[pl.ds(d * pad, pad), pl.ds(0, lanes)].astype(F32)
            line = jnp.where(at // pad == d, block[own + digit : own + digit + 1], line)
        digits.append(line)
    txt_ids = (digits[0] + 256.0 * digits[1]).astype(jnp.int32)
    for copy in img_copies:
        copy.wait_recv()

    photos, texts = img_all[...], txt_all[...]
    logits = multiplier * lax.dot_general(
        photos, texts, (((1,), (1,)), ((), ())), preferred_element_type=F32
    ) + offset
    match = img_ids == txt_ids
    weights = jnp.where(match, -multiplier, multiplier) * jax.nn.sigmoid(
        jnp.where(match, -logits, logits)
    )
    real = (entry < own) & (lax.rem(at, pad) < own)
    weights = jnp.where(real, weights, 0.0).astype(BF16)

    img_sum = jnp.dot(weights, texts, preferred_element_type=F32)
    img_part[...] = img_sum.astype(BF16)
    img_backs = [
        send(img_part.at[pl.ds(d * pad, pad)], img_in, d, (img_back, img_got), (row, col_peer[d][1]))
        for d in range(1, n_col)
    ]
    for copy in reversed(img_backs):
        copy.start()
    txt_sum = lax.dot_general(
        weights, photos, (((0,), (0,)), ((), ())), preferred_element_type=F32
    )
    txt_part[...] = txt_sum.astype(BF16)
    txt_backs = [
        send(txt_part.at[pl.ds(d * pad, pad)], txt_in, d, (txt_back, txt_got), (row_peer[d][1], col))
        for d in range(1, n_row)
    ]
    for copy in reversed(txt_backs):
        copy.start()

    def finish(grad, total, copies, arrived, unit, scale):
        for d, copy in enumerate(copies, 1):
            copy.wait_recv()
            total = total + arrived[pl.ds(d * pad, pad)].astype(F32)
        grad[...] = back_through(unit[pl.ds(0, own)], scale, total[:own])

    finish(txt_grad, txt_sum[:pad], txt_backs, txt_in, txt_unit, txt_scale)
    finish(img_grad, img_sum[:pad], img_backs, img_in, img_unit, img_scale)
    for copy in txt_copies + img_copies + img_backs + txt_backs:
        copy.wait_send()


def solution(mesh):
    n_row, n_col = mesh.shape["row"], mesh.shape["col"]
    placed = (P(("row", "col"), None), P(("row", "col"), None), P(("row", "col")), P(), P())

    def shards(photo_features, sentence_features, described_photo_number, multiplier, offset):
        own, width = photo_features.shape
        pad = -(-(own + 2) // TILE) * TILE
        smem = pl.BlockSpec(memory_space=pltpu.SMEM)
        hbm = pl.BlockSpec(memory_space=pl.ANY)
        vmem = pl.BlockSpec(memory_space=pltpu.VMEM)
        grad = jax.ShapeDtypeStruct((own, width), F32)
        dma = pltpu.SemaphoreType.DMA
        return pl.pallas_call(
            functools.partial(kernel, n_row, n_col, own, pad),
            out_shape=(grad, grad),
            in_specs=[smem, smem, smem, hbm, hbm],
            out_specs=(vmem, vmem),
            scratch_shapes=[
                pltpu.VMEM((own, width), BF16),
                pltpu.VMEM((own, width), BF16),
                pltpu.VMEM((pad, width), F32),
                pltpu.VMEM((pad, width), F32),
                pltpu.VMEM((n_col * pad, width), BF16),
                pltpu.VMEM((n_row * pad, width), BF16),
                pltpu.VMEM((n_col * pad, width), BF16),
                pltpu.VMEM((n_row * pad, width), BF16),
                pltpu.VMEM((n_col * pad, width), BF16),
                pltpu.VMEM((n_row * pad, width), BF16),
                dma((2,)),
                dma((n_col,)), dma((n_col,)), dma((n_row,)), dma((n_row,)),
                dma((n_col,)), dma((n_col,)), dma((n_row,)), dma((n_row,)),
            ],
            compiler_params=pltpu.CompilerParams(
                collective_id=0, has_side_effects=True, vmem_limit_bytes=48 * 2**20
            ),
        )(
            described_photo_number, multiplier.reshape(1), offset.reshape(1),
            photo_features, sentence_features,
        )

    return jax.shard_map(
        shards,
        mesh=mesh,
        in_specs=placed,
        out_specs=(P(("row", "col"), None), P(("row", "col"), None)),
        check_vma=False,
    )
```

```python
import functools

import jax
import jax.numpy as jnp
from jax import lax
from jax.experimental import pallas as pl
from jax.experimental.pallas import tpu as pltpu
from jax.sharding import PartitionSpec as P

MESH = pl.DeviceIdType.MESH
TILE = 16
F32 = jnp.float32
BF16 = jnp.bfloat16


def partner(me, step, count):
    if count & (count - 1):
        return lax.rem(me + step, count), lax.rem(me + count - step, count)
    bit = 1
    peer = me
    while bit <= step:
        if step & bit:
            peer = peer + bit * (1 - 2 * lax.rem(me // bit, 2))
        bit *= 2
    return peer, peer


def unit_rows(values):
    scale = lax.rsqrt(jnp.sum(values * values, axis=1, keepdims=True) + 1e-06)
    return values * scale, scale


def back_through(unit, scale, upstream):
    inner = jnp.sum(unit * upstream, axis=1, keepdims=True)
    return scale * (upstream - unit * inner)


def kernel(
    n_row, n_col, own, pad,
    ids_hbm, mul_hbm, off_hbm, img_hbm, txt_hbm, img_grad, txt_grad,
    ids_ref, mul_ref, off_ref, img_raw, txt_raw, img_unit, txt_unit, img_all, txt_all, img_part, txt_part, img_in, txt_in,
    load_sem, img_send, img_recv, txt_send, txt_recv, img_back, img_got, txt_back, txt_got,
):
    row, col = lax.axis_index("row"), lax.axis_index("col")
    loads = [
        pltpu.make_async_copy(img_hbm, img_raw, load_sem.at[0]),
        pltpu.make_async_copy(txt_hbm, txt_raw, load_sem.at[1]),
        pltpu.make_async_copy(ids_hbm, ids_ref, load_sem.at[2]),
        pltpu.make_async_copy(mul_hbm, mul_ref, load_sem.at[3]),
        pltpu.make_async_copy(off_hbm, off_ref, load_sem.at[4]),
    ]
    for load in loads:
        load.start()

    col_peer = [None] + [partner(col, d, n_col) for d in range(1, n_col)]
    row_peer = [None] + [partner(row, d, n_row) for d in range(1, n_row)]
    barrier = pltpu.get_barrier_semaphore()
    for d in range(1, n_col):
        pl.semaphore_signal(barrier, inc=1, device_id=(row, col_peer[d][1]), device_id_type=MESH)
    for d in range(1, n_row):
        pl.semaphore_signal(barrier, inc=1, device_id=(row_peer[d][1], col), device_id_type=MESH)

    width = img_raw.shape[1]
    lanes = n_row * pad
    lane = lax.rem(lax.broadcasted_iota(jnp.int32, (1, width), 1), pad)
    numbers = jnp.zeros((1, width), jnp.int32)
    loads[2].wait()
    for t in range(own):
        numbers = jnp.where(lane == t, ids_ref[t], numbers)
    low = lax.rem(numbers, 256).astype(F32)
    high = (numbers // 256).astype(F32)

    loads[1].wait()
    txt_value, txt_scale = unit_rows(txt_raw[...].astype(F32))
    txt_unit[pl.ds(0, own)] = txt_value
    txt_unit[pl.ds(own, 1)] = low
    txt_unit[pl.ds(own + 1, 1)] = high
    txt_unit[pl.ds(own + 2, pad - own - 2)] = jnp.zeros((pad - own - 2, width), F32)
    txt_all[pl.ds(0, pad)] = txt_unit[...].astype(BF16)
    loads[0].wait()
    img_value, img_scale = unit_rows(img_raw[...].astype(F32))
    img_unit[pl.ds(0, own)] = img_value
    img_unit[pl.ds(own, pad - own)] = jnp.zeros((pad - own, width), F32)
    img_all[pl.ds(0, pad)] = img_unit[...].astype(BF16)

    pl.semaphore_wait(barrier, n_col + n_row - 2)

    def send(src, dst, d, sems, peer):
        return pltpu.make_async_remote_copy(
            src_ref=src, dst_ref=dst.at[pl.ds(d * pad, pad)],
            send_sem=sems[0].at[d], recv_sem=sems[1].at[d],
            device_id=peer, device_id_type=MESH,
        )

    txt_copies = [
        send(txt_all.at[pl.ds(0, pad)], txt_all, d, (txt_send, txt_recv), (row_peer[d][0], col))
        for d in range(1, n_row)
    ]
    img_copies = [
        send(img_all.at[pl.ds(0, pad)], img_all, d, (img_send, img_recv), (row, col_peer[d][0]))
        for d in range(1, n_col)
    ]
    for copy in reversed(txt_copies):
        copy.start()
    for copy in reversed(img_copies):
        copy.start()

    loads[3].wait()
    loads[4].wait()
    multiplier, offset = mul_ref[0], off_ref[0]
    place = lax.broadcasted_iota(jnp.int32, (n_col * pad, 1), 0)
    slot, entry = place // pad, lax.rem(place, pad)
    owner = jnp.zeros((n_col * pad, 1), jnp.int32) + col
    for d in range(1, n_col):
        owner = jnp.where(slot == d, col_peer[d][1], owner)
    img_ids = (row * n_col + owner) * own + entry
    at = lax.broadcasted_iota(jnp.int32, (1, lanes), 1)

    for copy in txt_copies:
        copy.wait_recv()
    digits = []
    for digit in range(2):
        line = jnp.zeros((1, lanes), F32)
        for d in range(n_row):
            block = txt_all[pl.ds(d * pad, pad), pl.ds(0, lanes)].astype(F32)
            line = jnp.where(at // pad == d, block[own + digit : own + digit + 1], line)
        digits.append(line)
    txt_ids = (digits[0] + 256.0 * digits[1]).astype(jnp.int32)
    for copy in img_copies:
        copy.wait_recv()

    photos, texts = img_all[...], txt_all[...]
    logits = multiplier * lax.dot_general(
        photos, texts, (((1,), (1,)), ((), ())), preferred_element_type=F32
    ) + offset
    match = img_ids == txt_ids
    weights = jnp.where(match, -multiplier, multiplier) * jax.nn.sigmoid(
        jnp.where(match, -logits, logits)
    )
    real = (entry < own) & (lax.rem(at, pad) < own)
    weights = jnp.where(real, weights, 0.0).astype(BF16)

    img_sum = jnp.dot(weights, texts, preferred_element_type=F32)
    img_part[...] = img_sum.astype(BF16)
    img_backs = [
        send(img_part.at[pl.ds(d * pad, pad)], img_in, d, (img_back, img_got), (row, col_peer[d][1]))
        for d in range(1, n_col)
    ]
    for copy in reversed(img_backs):
        copy.start()
    txt_sum = lax.dot_general(
        weights, photos, (((0,), (0,)), ((), ())), preferred_element_type=F32
    )
    txt_part[...] = txt_sum.astype(BF16)
    txt_backs = [
        send(txt_part.at[pl.ds(d * pad, pad)], txt_in, d, (txt_back, txt_got), (row_peer[d][1], col))
        for d in range(1, n_row)
    ]
    for copy in reversed(txt_backs):
        copy.start()

    def finish(grad, total, copies, arrived, unit, scale):
        for d, copy in enumerate(copies, 1):
            copy.wait_recv()
            total = total + arrived[pl.ds(d * pad, pad)].astype(F32)
        grad[...] = back_through(unit[pl.ds(0, own)], scale, total[:own])

    finish(txt_grad, txt_sum[:pad], txt_backs, txt_in, txt_unit, txt_scale)
    finish(img_grad, img_sum[:pad], img_backs, img_in, img_unit, img_scale)
    for copy in txt_copies + img_copies + img_backs + txt_backs:
        copy.wait_send()


def solution(mesh):
    n_row, n_col = mesh.shape["row"], mesh.shape["col"]
    placed = (P(("row", "col"), None), P(("row", "col"), None), P(("row", "col")), P(), P())

    def shards(photo_features, sentence_features, described_photo_number, multiplier, offset):
        own, width = photo_features.shape
        pad = -(-(own + 2) // TILE) * TILE
        hbm = pl.BlockSpec(memory_space=pltpu.HBM)
        vmem = pl.BlockSpec(memory_space=pltpu.VMEM)
        grad = pltpu.VMEM((own, width), F32)
        dma = pltpu.SemaphoreType.DMA
        return pl.pallas_call(
            functools.partial(kernel, n_row, n_col, own, pad),
            out_shape=(grad, grad),
            in_specs=[hbm] * 5,
            out_specs=(vmem, vmem),
            scratch_shapes=[
                pltpu.SMEM((own,), jnp.int32),
                pltpu.SMEM((1,), F32),
                pltpu.SMEM((1,), F32),
                pltpu.VMEM((own, width), BF16),
                pltpu.VMEM((own, width), BF16),
                pltpu.VMEM((pad, width), F32),
                pltpu.VMEM((pad, width), F32),
                pltpu.VMEM((n_col * pad, width), BF16),
                pltpu.VMEM((n_row * pad, width), BF16),
                pltpu.VMEM((n_col * pad, width), BF16),
                pltpu.VMEM((n_row * pad, width), BF16),
                pltpu.VMEM((n_col * pad, width), BF16),
                pltpu.VMEM((n_row * pad, width), BF16),
                dma((5,)),
                dma((n_col,)), dma((n_col,)), dma((n_row,)), dma((n_row,)),
                dma((n_col,)), dma((n_col,)), dma((n_row,)), dma((n_row,)),
            ],
            compiler_params=pltpu.CompilerParams(
                collective_id=0, has_side_effects=True, vmem_limit_bytes=60 * 2**20
            ),
        )(
            described_photo_number, multiplier.reshape(1), offset.reshape(1),
            photo_features, sentence_features,
        )

    return jax.shard_map(
        shards,
        mesh=mesh,
        in_specs=placed,
        out_specs=(P(("row", "col"), None), P(("row", "col"), None)),
        check_vma=False,
    )
```

```python
import functools

import jax
import jax.numpy as jnp
from jax import lax
from jax.experimental import pallas as pl
from jax.experimental.pallas import tpu as pltpu
from jax.sharding import PartitionSpec as P

MESH = pl.DeviceIdType.MESH
PAD, OWN, QUAD, LANES = 16, 12, 4, 128
F32 = jnp.float32
BF16 = jnp.bfloat16


def spots(main):
    return [
        (QUAD * q, LANES * h, LANES * (3 * h + q)) for h in range(2) for q in range(3)
    ]


def partner(me, step, count):
    if count & (count - 1):
        return lax.rem(me + step, count), lax.rem(me + count - step, count)
    bit = 1
    peer = me
    while bit <= step:
        if step & bit:
            peer = peer + bit * (1 - 2 * lax.rem(me // bit, 2))
        bit *= 2
    return peer, peer


def unit_rows(values):
    scale = lax.rsqrt(jnp.sum(values * values, axis=1, keepdims=True) + 1e-06)
    return values * scale, scale


def back_through(unit, scale, upstream):
    inner = jnp.sum(unit * upstream, axis=1, keepdims=True)
    return scale * (upstream - unit * inner)


def kernel(
    n_row, n_col,
    mul_ref, off_ref, ids_hbm, img_hbm, txt_hbm, img_grad, txt_grad,
    ids_ref, img_raw, txt_raw, img_unit, txt_unit,
    img_all, txt_all, img_tail, txt_tail, img_sum, txt_sum, img_part, txt_part, img_in, txt_in,
    load_sem, img_send, img_recv, txt_send, txt_recv, img_back, img_got, txt_back, txt_got,
):
    row, col = lax.axis_index("row"), lax.axis_index("col")
    loads = [
        pltpu.make_async_copy(txt_hbm, txt_raw, load_sem.at[0]),
        pltpu.make_async_copy(img_hbm, img_raw, load_sem.at[1]),
        pltpu.make_async_copy(ids_hbm, ids_ref, load_sem.at[2]),
    ]
    for load in loads:
        load.start()

    col_peer = [None] + [partner(col, d, n_col) for d in range(1, n_col)]
    row_peer = [None] + [partner(row, d, n_row) for d in range(1, n_row)]
    barrier = pltpu.get_barrier_semaphore()
    for d in range(1, n_col):
        pl.semaphore_signal(barrier, inc=1, device_id=(row, col_peer[d][1]), device_id_type=MESH)
    for d in range(1, n_row):
        pl.semaphore_signal(barrier, inc=1, device_id=(row_peer[d][1], col), device_id_type=MESH)

    width = img_raw.shape[1]
    main = img_all.shape[1]
    rest = width - main
    places = spots(main)

    place = lax.broadcasted_iota(jnp.int32, (n_col * PAD, 1), 0)
    slot, entry = place // PAD, lax.rem(place, PAD)
    owner = jnp.zeros((n_col * PAD, 1), jnp.int32) + col
    for d in range(1, n_col):
        owner = jnp.where(slot == d, col_peer[d][1], owner)
    img_ids = (row * n_col + owner) * OWN + entry
    at = lax.broadcasted_iota(jnp.int32, (1, n_row * PAD), 1)
    real = (entry < OWN) & (lax.rem(at, PAD) < OWN)
    zeros = jnp.zeros((PAD - OWN, rest), F32)
    for tail, count in ((img_tail, n_col), (txt_tail, n_row)):
        for d in range(count):
            tail[pl.ds(d * PAD + OWN, PAD - OWN)] = zeros

    loads[2].wait()
    lane = lax.rem(lax.broadcasted_iota(jnp.int32, (1, LANES), 1), PAD)
    numbers = jnp.zeros((1, LANES), jnp.int32)
    for t in range(OWN):
        numbers = jnp.where(lane == t, ids_ref[t], numbers)
    low = lax.rem(numbers, 256).astype(F32)
    high = (numbers // 256).astype(F32)

    def pack(raw, unit, whole, tail, packed):
        value, scale = unit_rows(raw[...].astype(F32))
        unit[...] = value
        tail[pl.ds(0, OWN)] = value[:, main:]
        packed[pl.ds(0, OWN)] = value[:, :main]
        for first, lanes, to in places:
            packed[pl.ds(OWN, QUAD), pl.ds(to, LANES)] = tail[
                pl.ds(first, QUAD), pl.ds(lanes, LANES)
            ]
        return scale

    free = pl.ds(main - LANES, LANES)
    loads[0].wait()
    txt_pack = txt_sum.at[pl.ds(0, PAD)]
    txt_scale = pack(txt_raw, txt_unit, txt_all, txt_tail, txt_pack)
    txt_pack[pl.ds(OWN, QUAD), free] = jnp.zeros((QUAD, LANES), F32)
    txt_pack[pl.ds(OWN, 1), free] = low
    txt_pack[pl.ds(OWN + 1, 1), free] = high
    txt_all[pl.ds(0, PAD)] = txt_pack[...].astype(BF16)
    loads[1].wait()
    img_pack = img_sum.at[pl.ds(0, PAD)]
    img_scale = pack(img_raw, img_unit, img_all, img_tail, img_pack)
    img_pack[pl.ds(OWN, QUAD), free] = jnp.zeros((QUAD, LANES), F32)
    img_all[pl.ds(0, PAD)] = img_pack[...].astype(BF16)

    pl.semaphore_wait(barrier, n_col + n_row - 2)

    def send(src, dst, d, sems, peer):
        return pltpu.make_async_remote_copy(
            src_ref=src, dst_ref=dst.at[pl.ds(d * PAD, PAD)],
            send_sem=sems[0].at[d], recv_sem=sems[1].at[d],
            device_id=peer, device_id_type=MESH,
        )

    txt_copies = [
        send(txt_all.at[pl.ds(0, PAD)], txt_all, d, (txt_send, txt_recv), (row_peer[d][0], col))
        for d in range(1, n_row)
    ]
    img_copies = [
        send(img_all.at[pl.ds(0, PAD)], img_all, d, (img_send, img_recv), (row, col_peer[d][0]))
        for d in range(1, n_col)
    ]
    for copy in reversed(txt_copies):
        copy.start()
    for copy in reversed(img_copies):
        copy.start()

    def unpack(whole, tail, d):
        block = whole[pl.ds(d * PAD, PAD), pl.ds(0, main - LANES)].astype(F32)
        for first, lanes, to in places:
            tail[pl.ds(d * PAD + first, QUAD), pl.ds(lanes, LANES)] = block[
                OWN:, to : to + LANES
            ]

    img_copies[0].wait_recv()
    unpack(img_all, img_tail, 1)
    for d, copy in enumerate(txt_copies, 1):
        copy.wait_recv()
        unpack(txt_all, txt_tail, d)
    digits = []
    for digit in range(2):
        line = jnp.zeros((1, n_row * PAD), F32)
        for d in range(n_row):
            block = txt_all[pl.ds(d * PAD, PAD), free].astype(F32)[OWN + digit : OWN + digit + 1]
            if n_row * PAD > LANES:
                block = jnp.concatenate([block] * (n_row * PAD // LANES), axis=1)
            line = jnp.where(at // PAD == d, block[:, : n_row * PAD], line)
        digits.append(line)
    txt_ids = (digits[0] + 256.0 * digits[1]).astype(jnp.int32)
    texts, text_tails = txt_all[...], txt_tail[...].astype(BF16)
    multiplier, offset = mul_ref[...], off_ref[...]
    for d, copy in enumerate(img_copies[1:], 2):
        copy.wait_recv()
        unpack(img_all, img_tail, d)

    photos, photo_tails = img_all[...], img_tail[...].astype(BF16)
    across = (((1,), (1,)), ((), ()))
    logits = multiplier * (
        lax.dot_general(photos, texts, across, preferred_element_type=F32)
        + lax.dot_general(photo_tails, text_tails, across, preferred_element_type=F32)
    ) + offset
    match = img_ids == txt_ids
    weights = jnp.where(match, -multiplier, multiplier) * jax.nn.sigmoid(
        jnp.where(match, -logits, logits)
    )
    weights = jnp.where(real, weights, 0.0).astype(BF16)

    def partial(head, tail, total, part, copies, count):
        total[...] = head
        for d in reversed(range(count)):
            for first, lanes, to in places:
                total[pl.ds(d * PAD + OWN, QUAD), pl.ds(to, LANES)] = tail[
                    d * PAD + first : d * PAD + first + QUAD, lanes : lanes + LANES
                ]
            if d:
                block = pl.ds(d * PAD, PAD)
                part[block] = total[block].astype(BF16)
                copies[d - 1].start()

    img_backs = [
        send(img_part.at[pl.ds(d * PAD, PAD)], img_in, d, (img_back, img_got), (row, col_peer[d][1]))
        for d in range(1, n_col)
    ]
    partial(
        jnp.dot(weights, texts, preferred_element_type=F32),
        jnp.dot(weights, text_tails, preferred_element_type=F32),
        img_sum, img_part, img_backs, n_col,
    )
    txt_backs = [
        send(txt_part.at[pl.ds(d * PAD, PAD)], txt_in, d, (txt_back, txt_got), (row_peer[d][1], col))
        for d in range(1, n_row)
    ]
    down = (((0,), (0,)), ((), ()))
    partial(
        lax.dot_general(weights, photos, down, preferred_element_type=F32),
        lax.dot_general(weights, photo_tails, down, preferred_element_type=F32),
        txt_sum, txt_part, txt_backs, n_row,
    )

    def finish(grad, total, copies, arrived, unit, scale):
        up = total[pl.ds(0, PAD)]
        for d, copy in enumerate(copies, 1):
            copy.wait_recv()
            up = up + arrived[pl.ds(d * PAD, PAD)].astype(F32)
        grad[:, pl.ds(0, main)] = up[:OWN]
        for first, lanes, to in places:
            grad[pl.ds(first, QUAD), pl.ds(main + lanes, LANES)] = up[OWN:, to : to + LANES]
        grad[...] = back_through(unit[...], scale, grad[...])

    finish(txt_grad, txt_sum, txt_backs, txt_in, txt_unit, txt_scale)
    finish(img_grad, img_sum, img_backs, img_in, img_unit, img_scale)
    for copy in txt_copies + img_copies + img_backs + txt_backs:
        copy.wait_send()


def store(img_ref, txt_ref, img_out, txt_out, sem):
    copies = [
        pltpu.make_async_copy(img_ref, img_out, sem.at[0]),
        pltpu.make_async_copy(txt_ref, txt_out, sem.at[1]),
    ]
    for copy in copies:
        copy.start()
    for copy in copies:
        copy.wait()


def solution(mesh):
    n_row, n_col = mesh.shape["row"], mesh.shape["col"]
    placed = (P(("row", "col"), None), P(("row", "col"), None), P(("row", "col")), P(), P())

    def shards(photo_features, sentence_features, described_photo_number, multiplier, offset):
        own, width = photo_features.shape
        assert own == OWN and width % LANES == 0
        main = width - 2 * LANES
        assert main == 7 * LANES
        smem = pl.BlockSpec(memory_space=pltpu.SMEM)
        hbm = pl.BlockSpec(memory_space=pltpu.HBM)
        vmem = pl.BlockSpec(memory_space=pltpu.VMEM)
        held = pltpu.VMEM((own, width), F32)
        dma = pltpu.SemaphoreType.DMA
        rows, cols = n_row * PAD, n_col * PAD
        grads = pl.pallas_call(
            functools.partial(kernel, n_row, n_col),
            out_shape=(held, held),
            in_specs=[smem, smem, hbm, hbm, hbm],
            out_specs=(vmem, vmem),
            scratch_shapes=[
                pltpu.SMEM((own,), jnp.int32),
                pltpu.VMEM((own, width), BF16),
                pltpu.VMEM((own, width), BF16),
                pltpu.VMEM((own, width), F32),
                pltpu.VMEM((own, width), F32),
                pltpu.VMEM((cols, main), BF16),
                pltpu.VMEM((rows, main), BF16),
                pltpu.VMEM((cols, width - main), F32),
                pltpu.VMEM((rows, width - main), F32),
                pltpu.VMEM((cols, main), F32),
                pltpu.VMEM((rows, main), F32),
                pltpu.VMEM((cols, main), BF16),
                pltpu.VMEM((rows, main), BF16),
                pltpu.VMEM((cols, main), BF16),
                pltpu.VMEM((rows, main), BF16),
                dma((3,)),
                dma((n_col,)), dma((n_col,)), dma((n_row,)), dma((n_row,)),
                dma((n_col,)), dma((n_col,)), dma((n_row,)), dma((n_row,)),
            ],
            compiler_params=pltpu.CompilerParams(
                collective_id=0, has_side_effects=True, vmem_limit_bytes=60 * 2**20
            ),
        )(multiplier, offset, described_photo_number, photo_features, sentence_features)
        grad = jax.ShapeDtypeStruct((own, width), F32)
        return pl.pallas_call(
            store,
            out_shape=(grad, grad),
            in_specs=[vmem, vmem],
            out_specs=(hbm, hbm),
            scratch_shapes=[dma((2,))],
        )(*grads)

    return jax.shard_map(
        shards,
        mesh=mesh,
        in_specs=placed,
        out_specs=(P(("row", "col"), None), P(("row", "col"), None)),
        check_vma=False,
    )
```

```python
import functools

import jax
import jax.numpy as jnp
from jax import lax
from jax.experimental import pallas as pl
from jax.experimental.pallas import tpu as pltpu
from jax.sharding import PartitionSpec as P

MESH = pl.DeviceIdType.MESH
PAD, OWN, QUAD, LANES = 16, 12, 4, 128
F32 = jnp.float32
BF16 = jnp.bfloat16


def spots(main):
    return [
        (QUAD * q, LANES * h, LANES * (3 * h + q)) for h in range(2) for q in range(3)
    ]


def partner(me, step, count):
    if count & (count - 1):
        return lax.rem(me + step, count), lax.rem(me + count - step, count)
    bit = 1
    peer = me
    while bit <= step:
        if step & bit:
            peer = peer + bit * (1 - 2 * lax.rem(me // bit, 2))
        bit *= 2
    return peer, peer


def unit_rows(values):
    scale = lax.rsqrt(jnp.sum(values * values, axis=1, keepdims=True) + 1e-06)
    return values * scale, scale


def back_through(unit, scale, upstream):
    inner = jnp.sum(unit * upstream, axis=1, keepdims=True)
    return scale * (upstream - unit * inner)


def kernel(
    n_row, n_col,
    mul_ref, off_ref, ids_hbm, img_hbm, txt_hbm, img_grad, txt_grad,
    ids_ref, img_raw, txt_raw, img_unit, txt_unit,
    img_all, txt_all, img_tail, txt_tail, img_sum, txt_sum, img_part, txt_part, img_in, txt_in,
    load_sem, img_send, img_recv, txt_send, txt_recv, img_back, img_got, txt_back, txt_got,
):
    row, col = lax.axis_index("row"), lax.axis_index("col")
    loads = [
        pltpu.make_async_copy(txt_hbm, txt_raw, load_sem.at[0]),
        pltpu.make_async_copy(img_hbm, img_raw, load_sem.at[1]),
        pltpu.make_async_copy(ids_hbm, ids_ref, load_sem.at[2]),
    ]
    for load in loads:
        load.start()

    col_peer = [None] + [partner(col, d, n_col) for d in range(1, n_col)]
    row_peer = [None] + [partner(row, d, n_row) for d in range(1, n_row)]
    barrier = pltpu.get_barrier_semaphore()
    for d in range(1, n_col):
        pl.semaphore_signal(barrier, inc=1, device_id=(row, col_peer[d][1]), device_id_type=MESH)
    for d in range(1, n_row):
        pl.semaphore_signal(barrier, inc=1, device_id=(row_peer[d][1], col), device_id_type=MESH)

    width = img_raw.shape[1]
    main = img_all.shape[1]
    rest = width - main
    places = spots(main)

    place = lax.broadcasted_iota(jnp.int32, (n_col * PAD, 1), 0)
    slot, entry = place // PAD, lax.rem(place, PAD)
    owner = jnp.zeros((n_col * PAD, 1), jnp.int32) + col
    for d in range(1, n_col):
        owner = jnp.where(slot == d, col_peer[d][1], owner)
    img_ids = (row * n_col + owner) * OWN + entry
    at = lax.broadcasted_iota(jnp.int32, (1, n_row * PAD), 1)
    real = (entry < OWN) & (lax.rem(at, PAD) < OWN)
    zeros = jnp.zeros((PAD - OWN, rest), F32)
    for tail, count in ((img_tail, n_col), (txt_tail, n_row)):
        for d in range(count):
            tail[pl.ds(d * PAD + OWN, PAD - OWN)] = zeros

    loads[2].wait()
    lane = lax.rem(lax.broadcasted_iota(jnp.int32, (1, LANES), 1), PAD)
    numbers = jnp.zeros((1, LANES), jnp.int32)
    for t in range(OWN):
        numbers = jnp.where(lane == t, ids_ref[t], numbers)
    low = lax.rem(numbers, 256).astype(F32)
    high = (numbers // 256).astype(F32)

    def pack(raw, unit, whole, tail, packed):
        value, scale = unit_rows(raw[...].astype(F32))
        unit[...] = value
        tail[pl.ds(0, OWN)] = value[:, main:]
        packed[pl.ds(0, OWN)] = value[:, :main]
        for first, lanes, to in places:
            packed[pl.ds(OWN, QUAD), pl.ds(to, LANES)] = tail[
                pl.ds(first, QUAD), pl.ds(lanes, LANES)
            ]
        return scale

    free = pl.ds(main - LANES, LANES)
    loads[0].wait()
    txt_pack = txt_sum.at[pl.ds(0, PAD)]
    txt_scale = pack(txt_raw, txt_unit, txt_all, txt_tail, txt_pack)
    txt_pack[pl.ds(OWN, QUAD), free] = jnp.zeros((QUAD, LANES), F32)
    txt_pack[pl.ds(OWN, 1), free] = low
    txt_pack[pl.ds(OWN + 1, 1), free] = high
    txt_all[pl.ds(0, PAD)] = txt_pack[...].astype(BF16)
    pl.semaphore_wait(barrier, n_col + n_row - 2)

    def send(src, dst, d, sems, peer):
        return pltpu.make_async_remote_copy(
            src_ref=src, dst_ref=dst.at[pl.ds(d * PAD, PAD)],
            send_sem=sems[0].at[d], recv_sem=sems[1].at[d],
            device_id=peer, device_id_type=MESH,
        )

    txt_copies = [
        send(txt_all.at[pl.ds(0, PAD)], txt_all, d, (txt_send, txt_recv), (row_peer[d][0], col))
        for d in range(1, n_row)
    ]
    for copy in reversed(txt_copies):
        copy.start()
    loads[1].wait()
    img_pack = img_sum.at[pl.ds(0, PAD)]
    img_scale = pack(img_raw, img_unit, img_all, img_tail, img_pack)
    img_pack[pl.ds(OWN, QUAD), free] = jnp.zeros((QUAD, LANES), F32)
    img_all[pl.ds(0, PAD)] = img_pack[...].astype(BF16)
    img_copies = [
        send(img_all.at[pl.ds(0, PAD)], img_all, d, (img_send, img_recv), (row, col_peer[d][0]))
        for d in range(1, n_col)
    ]
    for copy in img_copies:
        copy.start()

    def unpack(whole, tail, d):
        block = whole[pl.ds(d * PAD, PAD), pl.ds(0, main - LANES)].astype(F32)
        for first, lanes, to in places:
            tail[pl.ds(d * PAD + first, QUAD), pl.ds(lanes, LANES)] = block[
                OWN:, to : to + LANES
            ]

    img_copies[0].wait_recv()
    unpack(img_all, img_tail, 1)
    for d, copy in enumerate(txt_copies, 1):
        copy.wait_recv()
        unpack(txt_all, txt_tail, d)
    digits = []
    for digit in range(2):
        line = jnp.zeros((1, n_row * PAD), F32)
        for d in range(n_row):
            block = txt_all[pl.ds(d * PAD, PAD), free].astype(F32)[OWN + digit : OWN + digit + 1]
            if n_row * PAD > LANES:
                block = jnp.concatenate([block] * (n_row * PAD // LANES), axis=1)
            line = jnp.where(at // PAD == d, block[:, : n_row * PAD], line)
        digits.append(line)
    txt_ids = (digits[0] + 256.0 * digits[1]).astype(jnp.int32)
    texts, text_tails = txt_all[...], txt_tail[...].astype(BF16)
    multiplier, offset = mul_ref[...], off_ref[...]
    across = (((1,), (1,)), ((), ()))
    down = (((0,), (0,)), ((), ()))

    def weigh(first, count):
        rows = pl.ds(first * PAD, count * PAD)
        logits = multiplier * (
            lax.dot_general(img_all[rows], texts, across, preferred_element_type=F32)
            + lax.dot_general(
                img_tail[rows].astype(BF16), text_tails, across, preferred_element_type=F32
            )
        ) + offset
        span = slice(first * PAD, (first + count) * PAD)
        match = img_ids[span] == txt_ids
        weights = jnp.where(match, -multiplier, multiplier) * jax.nn.sigmoid(
            jnp.where(match, -logits, logits)
        )
        return jnp.where(real[span], weights, 0.0).astype(BF16)

    def partial(head, tail, total, part, copies, start, count):
        total[pl.ds(start * PAD, count * PAD)] = head
        for d in reversed(range(count)):
            for first, lanes, to in places:
                total[pl.ds((start + d) * PAD + OWN, QUAD), pl.ds(to, LANES)] = tail[
                    d * PAD + first : d * PAD + first + QUAD, lanes : lanes + LANES
                ]
            if start + d:
                block = pl.ds((start + d) * PAD, PAD)
                part[block] = total[block].astype(BF16)
                copies[start + d - 1].start()

    img_backs = [
        send(img_part.at[pl.ds(d * PAD, PAD)], img_in, d, (img_back, img_got), (row, col_peer[d][1]))
        for d in range(1, n_col)
    ]
    txt_backs = [
        send(txt_part.at[pl.ds(d * PAD, PAD)], txt_in, d, (txt_back, txt_got), (row_peer[d][1], col))
        for d in range(1, n_row)
    ]

    def img_partial(weights, first, count):
        partial(
            jnp.dot(weights, texts, preferred_element_type=F32),
            jnp.dot(weights, text_tails, preferred_element_type=F32),
            img_sum, img_part, img_backs, first, count,
        )

    half = n_col // 2
    for d in range(2, half):
        img_copies[d - 1].wait_recv()
        unpack(img_all, img_tail, d)
    near = weigh(0, half)
    img_partial(near, 0, half)
    for d in range(half, n_col):
        img_copies[d - 1].wait_recv()
        unpack(img_all, img_tail, d)
    far = weigh(half, n_col - half)
    weights = jnp.concatenate([near, far], axis=0)
    partial(
        lax.dot_general(weights, img_all[...], down, preferred_element_type=F32),
        lax.dot_general(weights, img_tail[...].astype(BF16), down, preferred_element_type=F32),
        txt_sum, txt_part, txt_backs, 0, n_row,
    )
    img_partial(far, half, n_col - half)

    def finish(grad, total, copies, arrived, unit, scale):
        up = total[pl.ds(0, PAD)]
        for d, copy in enumerate(copies, 1):
            copy.wait_recv()
            up = up + arrived[pl.ds(d * PAD, PAD)].astype(F32)
        grad[:, pl.ds(0, main)] = up[:OWN]
        for first, lanes, to in places:
            grad[pl.ds(first, QUAD), pl.ds(main + lanes, LANES)] = up[OWN:, to : to + LANES]
        grad[...] = back_through(unit[...], scale, grad[...])

    finish(txt_grad, txt_sum, txt_backs, txt_in, txt_unit, txt_scale)
    finish(img_grad, img_sum, img_backs, img_in, img_unit, img_scale)
    for copy in txt_copies + img_copies + img_backs + txt_backs:
        copy.wait_send()


def store(img_ref, txt_ref, img_out, txt_out, sem):
    copies = [
        pltpu.make_async_copy(img_ref, img_out, sem.at[0]),
        pltpu.make_async_copy(txt_ref, txt_out, sem.at[1]),
    ]
    for copy in copies:
        copy.start()
    for copy in copies:
        copy.wait()


def solution(mesh):
    n_row, n_col = mesh.shape["row"], mesh.shape["col"]
    placed = (P(("row", "col"), None), P(("row", "col"), None), P(("row", "col")), P(), P())

    def shards(photo_features, sentence_features, described_photo_number, multiplier, offset):
        own, width = photo_features.shape
        assert own == OWN and width % LANES == 0
        main = width - 2 * LANES
        assert main == 7 * LANES
        smem = pl.BlockSpec(memory_space=pltpu.SMEM)
        hbm = pl.BlockSpec(memory_space=pltpu.HBM)
        vmem = pl.BlockSpec(memory_space=pltpu.VMEM)
        held = pltpu.VMEM((own, width), F32)
        dma = pltpu.SemaphoreType.DMA
        rows, cols = n_row * PAD, n_col * PAD
        grads = pl.pallas_call(
            functools.partial(kernel, n_row, n_col),
            out_shape=(held, held),
            in_specs=[smem, smem, hbm, hbm, hbm],
            out_specs=(vmem, vmem),
            scratch_shapes=[
                pltpu.SMEM((own,), jnp.int32),
                pltpu.VMEM((own, width), BF16),
                pltpu.VMEM((own, width), BF16),
                pltpu.VMEM((own, width), F32),
                pltpu.VMEM((own, width), F32),
                pltpu.VMEM((cols, main), BF16),
                pltpu.VMEM((rows, main), BF16),
                pltpu.VMEM((cols, width - main), F32),
                pltpu.VMEM((rows, width - main), F32),
                pltpu.VMEM((cols, main), F32),
                pltpu.VMEM((rows, main), F32),
                pltpu.VMEM((cols, main), BF16),
                pltpu.VMEM((rows, main), BF16),
                pltpu.VMEM((cols, main), BF16),
                pltpu.VMEM((rows, main), BF16),
                dma((3,)),
                dma((n_col,)), dma((n_col,)), dma((n_row,)), dma((n_row,)),
                dma((n_col,)), dma((n_col,)), dma((n_row,)), dma((n_row,)),
            ],
            compiler_params=pltpu.CompilerParams(
                collective_id=0, has_side_effects=True, vmem_limit_bytes=60 * 2**20
            ),
        )(multiplier, offset, described_photo_number, photo_features, sentence_features)
        grad = jax.ShapeDtypeStruct((own, width), F32)
        return pl.pallas_call(
            store,
            out_shape=(grad, grad),
            in_specs=[vmem, vmem],
            out_specs=(hbm, hbm),
            scratch_shapes=[dma((2,))],
            compiler_params=pltpu.CompilerParams(vmem_limit_bytes=2**20),
        )(*grads)

    return jax.shard_map(
        shards,
        mesh=mesh,
        in_specs=placed,
        out_specs=(P(("row", "col"), None), P(("row", "col"), None)),
        check_vma=False,
    )
```

```python
import functools

import jax
import jax.numpy as jnp
from jax import lax
from jax.experimental import pallas as pl
from jax.experimental.pallas import tpu as pltpu
from jax.sharding import PartitionSpec as P

MESH = pl.DeviceIdType.MESH
PAD, OWN, QUAD, LANES = 16, 12, 4, 128
F32 = jnp.float32
BF16 = jnp.bfloat16


def spots(main):
    return [
        (QUAD * q, LANES * h, LANES * (3 * h + q)) for h in range(2) for q in range(3)
    ]


def partner(me, step, count):
    if count & (count - 1):
        return lax.rem(me + step, count), lax.rem(me + count - step, count)
    bit = 1
    peer = me
    while bit <= step:
        if step & bit:
            peer = peer + bit * (1 - 2 * lax.rem(me // bit, 2))
        bit *= 2
    return peer, peer


def unit_rows(values):
    scale = lax.rsqrt(jnp.sum(values * values, axis=1, keepdims=True) + 1e-06)
    return values * scale, scale


def back_through(unit, scale, upstream):
    inner = jnp.sum(unit * upstream, axis=1, keepdims=True)
    return scale * (upstream - unit * inner)


def kernel(
    n_row, n_col,
    mul_ref, off_ref, ids_hbm, img_hbm, txt_hbm, img_grad, txt_grad,
    ids_ref, img_raw, txt_raw, img_unit, txt_unit,
    img_all, txt_all, img_tail, txt_tail, img_sum, txt_sum, img_part, txt_part, img_in, txt_in,
    load_sem, img_send, img_recv, txt_send, txt_recv, img_back, img_got, txt_back, txt_got,
):
    row, col = lax.axis_index("row"), lax.axis_index("col")
    loads = [
        pltpu.make_async_copy(txt_hbm, txt_raw, load_sem.at[0]),
        pltpu.make_async_copy(img_hbm, img_raw, load_sem.at[1]),
        pltpu.make_async_copy(ids_hbm, ids_ref, load_sem.at[2]),
    ]
    for load in loads:
        load.start()

    col_peer = [None] + [partner(col, d, n_col) for d in range(1, n_col)]
    row_peer = [None] + [partner(row, d, n_row) for d in range(1, n_row)]
    barrier = pltpu.get_barrier_semaphore()
    for d in range(1, n_col):
        pl.semaphore_signal(barrier, inc=1, device_id=(row, col_peer[d][1]), device_id_type=MESH)
    for d in range(1, n_row):
        pl.semaphore_signal(barrier, inc=1, device_id=(row_peer[d][1], col), device_id_type=MESH)

    width = img_raw.shape[1]
    main = img_all.shape[1]
    rest = width - main
    places = spots(main)

    place = lax.broadcasted_iota(jnp.int32, (n_col * PAD, 1), 0)
    slot, entry = place // PAD, lax.rem(place, PAD)
    owner = jnp.zeros((n_col * PAD, 1), jnp.int32) + col
    for d in range(1, n_col):
        owner = jnp.where(slot == d, col_peer[d][1], owner)
    img_ids = (row * n_col + owner) * OWN + entry
    at = lax.broadcasted_iota(jnp.int32, (1, n_row * PAD), 1)
    real = (entry < OWN) & (lax.rem(at, PAD) < OWN)
    zeros = jnp.zeros((PAD - OWN, rest), F32)
    for tail, count in ((img_tail, n_col), (txt_tail, n_row)):
        for d in range(count):
            tail[pl.ds(d * PAD + OWN, PAD - OWN)] = zeros

    loads[2].wait()
    lane = lax.rem(lax.broadcasted_iota(jnp.int32, (1, LANES), 1), PAD)
    numbers = jnp.zeros((1, LANES), jnp.int32)
    for t in range(OWN):
        numbers = jnp.where(lane == t, ids_ref[t], numbers)
    low = lax.rem(numbers, 256).astype(F32)
    high = (numbers // 256).astype(F32)

    loads[0].wait()
    loads[1].wait()
    txt_value, txt_scale = unit_rows(txt_raw[...].astype(F32))
    img_value, img_scale = unit_rows(img_raw[...].astype(F32))
    txt_unit[...] = txt_value
    img_unit[...] = img_value
    free = pl.ds(main - LANES, LANES)
    txt_sum[pl.ds(OWN, QUAD), free] = jnp.concatenate([low, high, low, high], axis=0)
    img_sum[pl.ds(OWN, QUAD), free] = jnp.zeros((QUAD, LANES), F32)
    for value, tail, packed in ((txt_value, txt_tail, txt_sum), (img_value, img_tail, img_sum)):
        tail[pl.ds(0, OWN)] = value[:, main:]
        packed[pl.ds(0, OWN)] = value[:, :main]
        for first, lanes, to in places:
            packed[pl.ds(OWN, QUAD), pl.ds(to, LANES)] = value[
                first : first + QUAD, main + lanes : main + lanes + LANES
            ]
    txt_all[pl.ds(0, PAD)] = txt_sum[pl.ds(0, PAD)].astype(BF16)
    img_all[pl.ds(0, PAD)] = img_sum[pl.ds(0, PAD)].astype(BF16)

    pl.semaphore_wait(barrier, n_col + n_row - 2)

    def send(src, dst, d, sems, peer):
        return pltpu.make_async_remote_copy(
            src_ref=src, dst_ref=dst.at[pl.ds(d * PAD, PAD)],
            send_sem=sems[0].at[d], recv_sem=sems[1].at[d],
            device_id=peer, device_id_type=MESH,
        )

    txt_copies = [
        send(txt_all.at[pl.ds(0, PAD)], txt_all, d, (txt_send, txt_recv), (row_peer[d][0], col))
        for d in range(1, n_row)
    ]
    img_copies = [
        send(img_all.at[pl.ds(0, PAD)], img_all, d, (img_send, img_recv), (row, col_peer[d][0]))
        for d in range(1, n_col)
    ]
    for copy in reversed(txt_copies):
        copy.start()
    for copy in reversed(img_copies):
        copy.start()

    def unpack(whole, tail, d):
        block = whole[pl.ds(d * PAD, PAD), pl.ds(0, main - LANES)].astype(F32)
        for first, lanes, to in places:
            tail[pl.ds(d * PAD + first, QUAD), pl.ds(lanes, LANES)] = block[
                OWN:, to : to + LANES
            ]

    img_copies[0].wait_recv()
    unpack(img_all, img_tail, 1)
    for d, copy in enumerate(txt_copies, 1):
        copy.wait_recv()
        unpack(txt_all, txt_tail, d)
    digits = []
    for digit in range(2):
        line = jnp.zeros((1, n_row * PAD), F32)
        for d in range(n_row):
            block = txt_all[pl.ds(d * PAD, PAD), free].astype(F32)[OWN + digit : OWN + digit + 1]
            if n_row * PAD > LANES:
                block = jnp.concatenate([block] * (n_row * PAD // LANES), axis=1)
            line = jnp.where(at // PAD == d, block[:, : n_row * PAD], line)
        digits.append(line)
    txt_ids = (digits[0] + 256.0 * digits[1]).astype(jnp.int32)
    texts, text_tails = txt_all[...], txt_tail[...].astype(BF16)
    multiplier, offset = mul_ref[...], off_ref[...]
    across = (((1,), (1,)), ((), ()))
    down = (((0,), (0,)), ((), ()))

    def weigh(first, count):
        rows = pl.ds(first * PAD, count * PAD)
        logits = multiplier * (
            lax.dot_general(img_all[rows], texts, across, preferred_element_type=F32)
            + lax.dot_general(
                img_tail[rows].astype(BF16), text_tails, across, preferred_element_type=F32
            )
        ) + offset
        span = slice(first * PAD, (first + count) * PAD)
        match = img_ids[span] == txt_ids
        weights = jnp.where(match, -multiplier, multiplier) * jax.nn.sigmoid(
            jnp.where(match, -logits, logits)
        )
        return jnp.where(real[span], weights, 0.0).astype(BF16)

    def partial(head, tail, total, part, copies, start, count):
        total[pl.ds(start * PAD, count * PAD)] = head
        for d in reversed(range(count)):
            for first, lanes, to in places:
                total[pl.ds((start + d) * PAD + OWN, QUAD), pl.ds(to, LANES)] = tail[
                    d * PAD + first : d * PAD + first + QUAD, lanes : lanes + LANES
                ]
            if start + d:
                block = pl.ds((start + d) * PAD, PAD)
                part[block] = total[block].astype(BF16)
                copies[start + d - 1].start()

    img_backs = [
        send(img_part.at[pl.ds(d * PAD, PAD)], img_in, d, (img_back, img_got), (row, col_peer[d][1]))
        for d in range(1, n_col)
    ]
    txt_backs = [
        send(txt_part.at[pl.ds(d * PAD, PAD)], txt_in, d, (txt_back, txt_got), (row_peer[d][1], col))
        for d in range(1, n_row)
    ]

    def img_partial(weights, first, count):
        partial(
            jnp.dot(weights, texts, preferred_element_type=F32),
            jnp.dot(weights, text_tails, preferred_element_type=F32),
            img_sum, img_part, img_backs, first, count,
        )

    for d in range(2, n_col):
        img_copies[d - 1].wait_recv()
        unpack(img_all, img_tail, d)
    weights = weigh(0, n_col)
    partial(
        lax.dot_general(weights, img_all[...], down, preferred_element_type=F32),
        lax.dot_general(weights, img_tail[...].astype(BF16), down, preferred_element_type=F32),
        txt_sum, txt_part, txt_backs, 0, n_row,
    )
    img_partial(weights, 0, n_col)

    def finish(grad, total, copies, arrived, unit, scale):
        up = total[pl.ds(0, PAD)]
        for d, copy in enumerate(copies, 1):
            copy.wait_recv()
            up = up + arrived[pl.ds(d * PAD, PAD)].astype(F32)
        grad[:, pl.ds(0, main)] = up[:OWN]
        for first, lanes, to in places:
            grad[pl.ds(first, QUAD), pl.ds(main + lanes, LANES)] = up[OWN:, to : to + LANES]
        grad[...] = back_through(unit[...], scale, grad[...])

    finish(txt_grad, txt_sum, txt_backs, txt_in, txt_unit, txt_scale)
    finish(img_grad, img_sum, img_backs, img_in, img_unit, img_scale)
    for copy in txt_copies + img_copies + img_backs + txt_backs:
        copy.wait_send()


def store(img_ref, txt_ref, img_out, txt_out, sem):
    copies = [
        pltpu.make_async_copy(img_ref, img_out, sem.at[0]),
        pltpu.make_async_copy(txt_ref, txt_out, sem.at[1]),
    ]
    for copy in copies:
        copy.start()
    for copy in copies:
        copy.wait()


def solution(mesh):
    n_row, n_col = mesh.shape["row"], mesh.shape["col"]
    placed = (P(("row", "col"), None), P(("row", "col"), None), P(("row", "col")), P(), P())

    def shards(photo_features, sentence_features, described_photo_number, multiplier, offset):
        own, width = photo_features.shape
        assert own == OWN and width % LANES == 0
        main = width - 2 * LANES
        assert main == 7 * LANES
        smem = pl.BlockSpec(memory_space=pltpu.SMEM)
        hbm = pl.BlockSpec(memory_space=pltpu.HBM)
        vmem = pl.BlockSpec(memory_space=pltpu.VMEM)
        held = pltpu.VMEM((own, width), F32)
        dma = pltpu.SemaphoreType.DMA
        rows, cols = n_row * PAD, n_col * PAD
        grads = pl.pallas_call(
            functools.partial(kernel, n_row, n_col),
            out_shape=(held, held),
            in_specs=[smem, smem, hbm, hbm, hbm],
            out_specs=(vmem, vmem),
            scratch_shapes=[
                pltpu.SMEM((own,), jnp.int32),
                pltpu.VMEM((own, width), BF16),
                pltpu.VMEM((own, width), BF16),
                pltpu.VMEM((own, width), F32),
                pltpu.VMEM((own, width), F32),
                pltpu.VMEM((cols, main), BF16),
                pltpu.VMEM((rows, main), BF16),
                pltpu.VMEM((cols, width - main), F32),
                pltpu.VMEM((rows, width - main), F32),
                pltpu.VMEM((cols, main), F32),
                pltpu.VMEM((rows, main), F32),
                pltpu.VMEM((cols, main), BF16),
                pltpu.VMEM((rows, main), BF16),
                pltpu.VMEM((cols, main), BF16),
                pltpu.VMEM((rows, main), BF16),
                dma((3,)),
                dma((n_col,)), dma((n_col,)), dma((n_row,)), dma((n_row,)),
                dma((n_col,)), dma((n_col,)), dma((n_row,)), dma((n_row,)),
            ],
            compiler_params=pltpu.CompilerParams(
                collective_id=0, has_side_effects=True, vmem_limit_bytes=60 * 2**20
            ),
        )(multiplier, offset, described_photo_number, photo_features, sentence_features)
        grad = jax.ShapeDtypeStruct((own, width), F32)
        return pl.pallas_call(
            store,
            out_shape=(grad, grad),
            in_specs=[vmem, vmem],
            out_specs=(hbm, hbm),
            scratch_shapes=[dma((2,))],
            compiler_params=pltpu.CompilerParams(vmem_limit_bytes=2**20),
        )(*grads)

    return jax.shard_map(
        shards,
        mesh=mesh,
        in_specs=placed,
        out_specs=(P(("row", "col"), None), P(("row", "col"), None)),
        check_vma=False,
    )
```

```python
import functools

import jax
import jax.numpy as jnp
from jax import lax
from jax.experimental import pallas as pl
from jax.experimental.pallas import tpu as pltpu
from jax.sharding import PartitionSpec as P

MESH = pl.DeviceIdType.MESH
PAD, LANES = 16, 128
F32 = jnp.float32
BF16 = jnp.bfloat16

def partner(me, step, count):
    if count & (count - 1):
        return lax.rem(me + step, count), lax.rem(me + count - step, count)
    bit = 1
    peer = me
    while bit <= step:
        if step & bit:
            peer = peer + bit * (1 - 2 * lax.rem(me // bit, 2))
        bit *= 2
    return peer, peer


def unit_rows(values):
    scale = lax.rsqrt(jnp.sum(values * values, axis=1, keepdims=True) + 1e-06)
    return values * scale, scale


def back_through(unit, scale, upstream):
    inner = jnp.sum(unit * upstream, axis=1, keepdims=True)
    return scale * (upstream - unit * inner)


def kernel(
    n_row, n_col, own,
    mul_ref, off_ref, ids_hbm, img_hbm, txt_hbm, img_grad, txt_grad,
    ids_ref, img_raw, txt_raw, numbers, img_unit, txt_unit, img_part, txt_part, img_in, txt_in,
    load_sem, ids_send, ids_recv,
    img_send, img_recv, txt_send, txt_recv, img_back, img_got, txt_back, txt_got,
):
    row, col = lax.axis_index("row"), lax.axis_index("col")
    loads = [
        pltpu.make_async_copy(ids_hbm, ids_ref, load_sem.at[0]),
        pltpu.make_async_copy(txt_hbm, txt_raw.at[0], load_sem.at[1]),
        pltpu.make_async_copy(img_hbm, img_raw.at[0], load_sem.at[2]),
    ]
    for load in loads:
        load.start()

    col_peer = [None] + [partner(col, d, n_col) for d in range(1, n_col)]
    row_peer = [None] + [partner(row, d, n_row) for d in range(1, n_row)]
    barrier = pltpu.get_barrier_semaphore()
    for d in range(1, n_col):
        pl.semaphore_signal(barrier, inc=1, device_id=(row, col_peer[d][1]), device_id_type=MESH)
    for d in range(1, n_row):
        pl.semaphore_signal(barrier, inc=1, device_id=(row_peer[d][1], col), device_id_type=MESH)
    pl.semaphore_wait(barrier, n_col + n_row - 2)

    def send(src, dst, d, sems, peer):
        return pltpu.make_async_remote_copy(
            src_ref=src, dst_ref=dst.at[d], send_sem=sems[0].at[d], recv_sem=sems[1].at[d],
            device_id=peer, device_id_type=MESH,
        )

    txt_copies = [
        send(txt_hbm, txt_raw, d, (txt_send, txt_recv), (row_peer[d][0], col))
        for d in range(1, n_row)
    ]
    img_copies = [
        send(img_hbm, img_raw, d, (img_send, img_recv), (row, col_peer[d][0]))
        for d in range(1, n_col)
    ]
    for copy in reversed(txt_copies):
        copy.start()
    for copy in reversed(img_copies):
        copy.start()

    loads[0].wait()
    lane = lax.rem(lax.broadcasted_iota(jnp.int32, numbers.shape[1:], 1), PAD)
    line = jnp.zeros(numbers.shape[1:], jnp.int32)
    for t in range(own):
        line = jnp.where(lane == t, ids_ref[t], line)
    numbers[0] = line
    ids_copies = [
        send(numbers.at[0], numbers, d, (ids_send, ids_recv), (row_peer[d][0], col))
        for d in range(1, n_row)
    ]
    for copy in ids_copies:
        copy.start()

    width = img_unit.shape[1]
    place = lax.broadcasted_iota(jnp.int32, (n_col * PAD, 1), 0)
    slot, entry = place // PAD, lax.rem(place, PAD)
    owner = jnp.zeros((n_col * PAD, 1), jnp.int32) + col
    for d in range(1, n_col):
        owner = jnp.where(slot == d, col_peer[d][1], owner)
    img_ids = (row * n_col + owner) * own + entry
    at = lax.broadcasted_iota(jnp.int32, (1, n_row * PAD), 1)
    real = (entry < own) & (lax.rem(at, PAD) < own)
    zeros = jnp.zeros((PAD - own, width), F32)
    for unit, count in ((img_unit, n_col), (txt_unit, n_row)):
        for d in range(count):
            unit[pl.ds(d * PAD + own, PAD - own)] = zeros

    def normalise(raw, unit, d):
        value, scale = unit_rows(raw[d].astype(F32))
        unit[pl.ds(d * PAD, own)] = value
        return scale

    loads[1].wait()
    txt_scale = normalise(txt_raw, txt_unit, 0)
    loads[2].wait()
    img_scale = normalise(img_raw, img_unit, 0)
    img_copies[0].wait_recv()
    normalise(img_raw, img_unit, 1)
    for d, copy in enumerate(txt_copies, 1):
        copy.wait_recv()
        normalise(txt_raw, txt_unit, d)
    for copy in ids_copies:
        copy.wait_recv()
    txt_ids = jnp.zeros((1, n_row * PAD), jnp.int32)
    for d in range(n_row):
        block = numbers[d][:1]
        if n_row * PAD > LANES:
            block = jnp.concatenate([block] * (n_row * PAD // LANES), axis=1)
        txt_ids = jnp.where(at // PAD == d, block[:, : n_row * PAD], txt_ids)
    for d in range(2, n_col):
        img_copies[d - 1].wait_recv()
        normalise(img_raw, img_unit, d)

    multiplier, offset = mul_ref[...], off_ref[...]
    texts, photos = txt_unit[...].astype(BF16), img_unit[...].astype(BF16)
    logits = multiplier * lax.dot_general(
        photos, texts, (((1,), (1,)), ((), ())), preferred_element_type=F32
    ) + offset
    match = img_ids == txt_ids
    weights = jnp.where(match, -multiplier, multiplier) * jax.nn.sigmoid(
        jnp.where(match, -logits, logits)
    )
    weights = jnp.where(real, weights, 0.0).astype(BF16)

    def partial(total, part, copies):
        for d, copy in reversed(list(enumerate(copies, 1))):
            part[d] = total[d * PAD : d * PAD + own].astype(BF16)
            copy.start()
        return total[:own]

    txt_backs = [
        send(txt_part.at[d], txt_in, d, (txt_back, txt_got), (row_peer[d][1], col))
        for d in range(1, n_row)
    ]
    img_backs = [
        send(img_part.at[d], img_in, d, (img_back, img_got), (row, col_peer[d][1]))
        for d in range(1, n_col)
    ]
    txt_up = partial(
        lax.dot_general(weights, photos, (((0,), (0,)), ((), ())), preferred_element_type=F32),
        txt_part, txt_backs,
    )
    img_up = partial(
        jnp.dot(weights, texts, preferred_element_type=F32), img_part, img_backs
    )

    def finish(grad, up, copies, arrived, unit, scale):
        for d, copy in enumerate(copies, 1):
            copy.wait_recv()
            up = up + arrived[d].astype(F32)
        grad[...] = back_through(unit[pl.ds(0, own)], scale, up)

    finish(txt_grad, txt_up, txt_backs, txt_in, txt_unit, txt_scale)
    finish(img_grad, img_up, img_backs, img_in, img_unit, img_scale)
    for copy in txt_copies + img_copies + ids_copies + img_backs + txt_backs:
        copy.wait_send()


def store(img_ref, txt_ref, img_out, txt_out, sem):
    copies = [
        pltpu.make_async_copy(img_ref, img_out, sem.at[0]),
        pltpu.make_async_copy(txt_ref, txt_out, sem.at[1]),
    ]
    for copy in copies:
        copy.start()
    for copy in copies:
        copy.wait()


def solution(mesh):
    n_row, n_col = mesh.shape["row"], mesh.shape["col"]
    placed = (P(("row", "col"), None), P(("row", "col"), None), P(("row", "col")), P(), P())

    def shards(photo_features, sentence_features, described_photo_number, multiplier, offset):
        own, width = photo_features.shape
        smem = pl.BlockSpec(memory_space=pltpu.SMEM)
        hbm = pl.BlockSpec(memory_space=pltpu.HBM)
        vmem = pl.BlockSpec(memory_space=pltpu.VMEM)
        held = pltpu.VMEM((own, width), F32)
        dma = pltpu.SemaphoreType.DMA
        rows, cols = n_row * PAD, n_col * PAD
        grads = pl.pallas_call(
            functools.partial(kernel, n_row, n_col, own),
            out_shape=(held, held),
            in_specs=[smem, smem, hbm, hbm, hbm],
            out_specs=(vmem, vmem),
            scratch_shapes=[
                pltpu.SMEM((own,), jnp.int32),
                pltpu.VMEM((n_col, own, width), BF16),
                pltpu.VMEM((n_row, own, width), BF16),
                pltpu.VMEM((n_row, 8, LANES), jnp.int32),
                pltpu.VMEM((cols, width), F32),
                pltpu.VMEM((rows, width), F32),
                pltpu.VMEM((n_col, own, width), BF16),
                pltpu.VMEM((n_row, own, width), BF16),
                pltpu.VMEM((n_col, own, width), BF16),
                pltpu.VMEM((n_row, own, width), BF16),
                dma((3,)), dma((n_row,)), dma((n_row,)),
                dma((n_col,)), dma((n_col,)), dma((n_row,)), dma((n_row,)),
                dma((n_col,)), dma((n_col,)), dma((n_row,)), dma((n_row,)),
            ],
            compiler_params=pltpu.CompilerParams(
                collective_id=0, has_side_effects=True, vmem_limit_bytes=60 * 2**20
            ),
        )(multiplier, offset, described_photo_number, photo_features, sentence_features)
        grad = jax.ShapeDtypeStruct((own, width), F32)
        return pl.pallas_call(
            store,
            out_shape=(grad, grad),
            in_specs=[vmem, vmem],
            out_specs=(hbm, hbm),
            scratch_shapes=[dma((2,))],
            compiler_params=pltpu.CompilerParams(vmem_limit_bytes=2**20),
        )(*grads)

    return jax.shard_map(
        shards,
        mesh=mesh,
        in_specs=placed,
        out_specs=(P(("row", "col"), None), P(("row", "col"), None)),
        check_vma=False,
    )
```

```python
import functools

import jax
import jax.numpy as jnp
from jax import lax
from jax.experimental import pallas as pl
from jax.experimental.pallas import tpu as pltpu
from jax.sharding import PartitionSpec as P

MESH = pl.DeviceIdType.MESH
PAD, OWN, QUAD, LANES = 16, 12, 4, 128
F32 = jnp.float32
BF16 = jnp.bfloat16


def spots(main):
    return [
        (QUAD * q, LANES * h, LANES * (3 * h + q)) for h in range(2) for q in range(3)
    ]


def partner(me, step, count):
    assert count & (count - 1) == 0
    bit = 1
    peer = me
    while bit <= step:
        if step & bit:
            peer = peer + bit * (1 - 2 * lax.rem(me // bit, 2))
        bit *= 2
    return peer, peer


def unit_rows(values):
    scale = lax.rsqrt(jnp.sum(values * values, axis=1, keepdims=True) + 1e-06)
    return values * scale, scale


def back_through(unit, scale, upstream):
    inner = jnp.sum(unit * upstream, axis=1, keepdims=True)
    return scale * (upstream - unit * inner)


def kernel(
    n_row, n_col,
    mul_ref, off_ref, ids_hbm, img_hbm, txt_hbm, img_grad, txt_grad,
    ids_ref, img_raw, txt_raw, img_unit, txt_unit,
    img_all, txt_all, img_tail, txt_tail, img_sum, txt_sum, img_part, txt_part, img_in, txt_in, img_mid,
    load_sem, mid_send, mid_recv, img_send, img_recv, txt_send, txt_recv, img_back, img_got, txt_back, txt_got,
):
    row, col = lax.axis_index("row"), lax.axis_index("col")
    loads = [
        pltpu.make_async_copy(txt_hbm, txt_raw, load_sem.at[0]),
        pltpu.make_async_copy(img_hbm, img_raw, load_sem.at[1]),
        pltpu.make_async_copy(ids_hbm, ids_ref, load_sem.at[2]),
    ]
    for load in loads:
        load.start()

    col_peer = [None] + [partner(col, d, n_col) for d in range(1, n_col)]
    row_peer = [None] + [partner(row, d, n_row) for d in range(1, n_row)]
    barrier = pltpu.get_barrier_semaphore()
    for d in range(1, n_col):
        pl.semaphore_signal(barrier, inc=1, device_id=(row, col_peer[d][1]), device_id_type=MESH)
    for d in range(1, n_row):
        pl.semaphore_signal(barrier, inc=1, device_id=(row_peer[d][1], col), device_id_type=MESH)

    width = img_raw.shape[1]
    main = img_all.shape[1]
    rest = width - main
    places = spots(main)

    place = lax.broadcasted_iota(jnp.int32, (n_col * PAD, 1), 0)
    slot, entry = place // PAD, lax.rem(place, PAD)
    owner = jnp.zeros((n_col * PAD, 1), jnp.int32) + col
    for d in range(1, n_col):
        owner = jnp.where(slot == d, col_peer[d][1], owner)
    img_ids = (row * n_col + owner) * OWN + entry
    at = lax.broadcasted_iota(jnp.int32, (1, n_row * PAD), 1)
    real = (entry < OWN) & (lax.rem(at, PAD) < OWN)
    zeros = jnp.zeros((PAD - OWN, rest), F32)
    for tail, count in ((img_tail, n_col), (txt_tail, n_row)):
        for d in range(count):
            tail[pl.ds(d * PAD + OWN, PAD - OWN)] = zeros

    loads[2].wait()
    lane = lax.rem(lax.broadcasted_iota(jnp.int32, (1, LANES), 1), PAD)
    numbers = jnp.zeros((1, LANES), jnp.int32)
    for t in range(OWN):
        numbers = jnp.where(lane == t, ids_ref[t], numbers)
    low = lax.rem(numbers, 256).astype(F32)
    high = (numbers // 256).astype(F32)

    loads[0].wait()
    loads[1].wait()
    txt_value, txt_scale = unit_rows(txt_raw[...].astype(F32))
    img_value, img_scale = unit_rows(img_raw[...].astype(F32))
    txt_unit[...] = txt_value
    img_unit[...] = img_value
    free = pl.ds(main - LANES, LANES)
    txt_sum[pl.ds(OWN, QUAD), free] = jnp.concatenate([low, high, low, high], axis=0)
    img_sum[pl.ds(OWN, QUAD), free] = jnp.zeros((QUAD, LANES), F32)
    for value, tail, packed in ((txt_value, txt_tail, txt_sum), (img_value, img_tail, img_sum)):
        tail[pl.ds(0, OWN)] = value[:, main:]
        packed[pl.ds(0, OWN)] = value[:, :main]
        for first, lanes, to in places:
            packed[pl.ds(OWN, QUAD), pl.ds(to, LANES)] = value[
                first : first + QUAD, main + lanes : main + lanes + LANES
            ]
    txt_all[pl.ds(0, PAD)] = txt_sum[pl.ds(0, PAD)].astype(BF16)
    img_all[pl.ds(0, PAD)] = img_sum[pl.ds(0, PAD)].astype(BF16)

    pl.semaphore_wait(barrier, n_col + n_row - 2)

    def send(src, dst, d, sems, peer):
        return pltpu.make_async_remote_copy(
            src_ref=src, dst_ref=dst.at[pl.ds(d * PAD, PAD)],
            send_sem=sems[0].at[d], recv_sem=sems[1].at[d],
            device_id=peer, device_id_type=MESH,
        )

    txt_copies = [
        send(txt_all.at[pl.ds(0, PAD)], txt_all, d, (txt_send, txt_recv), (row_peer[d][0], col))
        for d in range(1, n_row)
    ]
    sibling = (row, col_peer[1][0])
    img_copies = {
        d: send(
            img_all.at[pl.ds((d - 1) * PAD if d % 2 else 0, PAD)], img_all, d,
            (img_send, img_recv), sibling if d % 2 else (row, col_peer[d][0]),
        )
        for d in range(1, n_col)
    }
    evens = list(range(2, n_col, 2))
    for copy in reversed(txt_copies):
        copy.start()
    for d in reversed(evens):
        img_copies[d].start()
    img_copies[1].start()

    def unpack(whole, tail, d):
        block = whole[pl.ds(d * PAD, PAD), pl.ds(0, main - LANES)].astype(F32)
        for first, lanes, to in places:
            tail[pl.ds(d * PAD + first, QUAD), pl.ds(lanes, LANES)] = block[
                OWN:, to : to + LANES
            ]

    for d in evens:
        img_copies[d].wait_recv()
        img_copies[d + 1].start()
    for d in [1] + evens:
        if d == 1:
            img_copies[d].wait_recv()
        unpack(img_all, img_tail, d)
    for d, copy in enumerate(txt_copies, 1):
        copy.wait_recv()
        unpack(txt_all, txt_tail, d)
    digits = []
    for digit in range(2):
        line = jnp.zeros((1, n_row * PAD), F32)
        for d in range(n_row):
            block = txt_all[pl.ds(d * PAD, PAD), free].astype(F32)[OWN + digit : OWN + digit + 1]
            if n_row * PAD > LANES:
                block = jnp.concatenate([block] * (n_row * PAD // LANES), axis=1)
            line = jnp.where(at // PAD == d, block[:, : n_row * PAD], line)
        digits.append(line)
    txt_ids = (digits[0] + 256.0 * digits[1]).astype(jnp.int32)
    texts, text_tails = txt_all[...], txt_tail[...].astype(BF16)
    multiplier, offset = mul_ref[...], off_ref[...]
    across = (((1,), (1,)), ((), ()))
    down = (((0,), (0,)), ((), ()))

    def weigh(first, count):
        rows = pl.ds(first * PAD, count * PAD)
        logits = multiplier * (
            lax.dot_general(img_all[rows], texts, across, preferred_element_type=F32)
            + lax.dot_general(
                img_tail[rows].astype(BF16), text_tails, across, preferred_element_type=F32
            )
        ) + offset
        span = slice(first * PAD, (first + count) * PAD)
        match = img_ids[span] == txt_ids
        weights = jnp.where(match, -multiplier, multiplier) * jax.nn.sigmoid(
            jnp.where(match, -logits, logits)
        )
        return jnp.where(real[span], weights, 0.0).astype(BF16)

    def spread(total, tail, d):
        for first, lanes, to in places:
            total[pl.ds(d * PAD + OWN, QUAD), pl.ds(to, LANES)] = tail[
                d * PAD + first : d * PAD + first + QUAD, lanes : lanes + LANES
            ]

    for d in evens:
        img_copies[d + 1].wait_recv()
        unpack(img_all, img_tail, d + 1)
    weights = weigh(0, n_col)

    txt_backs = [
        send(txt_part.at[pl.ds(d * PAD, PAD)], txt_in, d, (txt_back, txt_got), (row_peer[d][1], col))
        for d in range(1, n_row)
    ]
    txt_sum[...] = lax.dot_general(weights, img_all[...], down, preferred_element_type=F32)
    tail = lax.dot_general(
        weights, img_tail[...].astype(BF16), down, preferred_element_type=F32
    )
    for d in reversed(range(n_row)):
        spread(txt_sum, tail, d)
        if d:
            block = pl.ds(d * PAD, PAD)
            txt_part[block] = txt_sum[block].astype(BF16)
            txt_backs[d - 1].start()

    mids = {
        d: send(img_part.at[pl.ds((d + 1) * PAD, PAD)], img_mid, d, (mid_send, mid_recv), sibling)
        for d in evens
    }
    img_backs = {
        d: send(
            img_part.at[pl.ds(d * PAD, PAD)], img_in, d, (img_back, img_got), (row, col_peer[d][1])
        )
        for d in [1] + evens
    }
    img_sum[...] = jnp.dot(weights, texts, preferred_element_type=F32)
    tail = jnp.dot(weights, text_tails, preferred_element_type=F32)
    for d in reversed(range(1, n_col, 2)):
        spread(img_sum, tail, d)
        block = pl.ds(d * PAD, PAD)
        img_part[block] = img_sum[block].astype(BF16)
        (mids[d - 1] if d > 1 else img_backs[1]).start()
    for d in reversed(range(0, n_col, 2)):
        spread(img_sum, tail, d)
    for d in reversed(evens):
        mids[d].wait_recv()
        block = pl.ds(d * PAD, PAD)
        img_part[block] = (img_sum[block] + img_mid[block].astype(F32)).astype(BF16)
        img_backs[d].start()

    def finish(grad, total, copies, arrived, unit, scale):
        up = total[pl.ds(0, PAD)]
        for d, copy in copies:
            copy.wait_recv()
            up = up + arrived[pl.ds(d * PAD, PAD)].astype(F32)
        grad[:, pl.ds(0, main)] = up[:OWN]
        for first, lanes, to in places:
            grad[pl.ds(first, QUAD), pl.ds(main + lanes, LANES)] = up[OWN:, to : to + LANES]
        grad[...] = back_through(unit[...], scale, grad[...])

    finish(txt_grad, txt_sum, list(enumerate(txt_backs, 1)), txt_in, txt_unit, txt_scale)
    finish(img_grad, img_sum, list(img_backs.items()), img_in, img_unit, img_scale)
    for copy in txt_copies + txt_backs:
        copy.wait_send()
    for group in (img_copies, mids, img_backs):
        for copy in group.values():
            copy.wait_send()


def store(img_ref, txt_ref, img_out, txt_out, sem):
    copies = [
        pltpu.make_async_copy(img_ref, img_out, sem.at[0]),
        pltpu.make_async_copy(txt_ref, txt_out, sem.at[1]),
    ]
    for copy in copies:
        copy.start()
    for copy in copies:
        copy.wait()


def solution(mesh):
    n_row, n_col = mesh.shape["row"], mesh.shape["col"]
    placed = (P(("row", "col"), None), P(("row", "col"), None), P(("row", "col")), P(), P())

    def shards(photo_features, sentence_features, described_photo_number, multiplier, offset):
        own, width = photo_features.shape
        assert own == OWN and width % LANES == 0
        main = width - 2 * LANES
        assert main == 7 * LANES
        smem = pl.BlockSpec(memory_space=pltpu.SMEM)
        hbm = pl.BlockSpec(memory_space=pltpu.HBM)
        vmem = pl.BlockSpec(memory_space=pltpu.VMEM)
        held = pltpu.VMEM((own, width), F32)
        dma = pltpu.SemaphoreType.DMA
        rows, cols = n_row * PAD, n_col * PAD
        grads = pl.pallas_call(
            functools.partial(kernel, n_row, n_col),
            out_shape=(held, held),
            in_specs=[smem, smem, hbm, hbm, hbm],
            out_specs=(vmem, vmem),
            scratch_shapes=[
                pltpu.SMEM((own,), jnp.int32),
                pltpu.VMEM((own, width), BF16),
                pltpu.VMEM((own, width), BF16),
                pltpu.VMEM((own, width), F32),
                pltpu.VMEM((own, width), F32),
                pltpu.VMEM((cols, main), BF16),
                pltpu.VMEM((rows, main), BF16),
                pltpu.VMEM((cols, width - main), F32),
                pltpu.VMEM((rows, width - main), F32),
                pltpu.VMEM((cols, main), F32),
                pltpu.VMEM((rows, main), F32),
                pltpu.VMEM((cols, main), BF16),
                pltpu.VMEM((rows, main), BF16),
                pltpu.VMEM((cols, main), BF16),
                pltpu.VMEM((rows, main), BF16),
                pltpu.VMEM((cols, main), BF16),
                dma((3,)), dma((n_col,)), dma((n_col,)),
                dma((n_col,)), dma((n_col,)), dma((n_row,)), dma((n_row,)),
                dma((n_col,)), dma((n_col,)), dma((n_row,)), dma((n_row,)),
            ],
            compiler_params=pltpu.CompilerParams(
                collective_id=0, has_side_effects=True, vmem_limit_bytes=60 * 2**20
            ),
        )(multiplier, offset, described_photo_number, photo_features, sentence_features)
        grad = jax.ShapeDtypeStruct((own, width), F32)
        return pl.pallas_call(
            store,
            out_shape=(grad, grad),
            in_specs=[vmem, vmem],
            out_specs=(hbm, hbm),
            scratch_shapes=[dma((2,))],
            compiler_params=pltpu.CompilerParams(vmem_limit_bytes=2**20),
        )(*grads)

    return jax.shard_map(
        shards,
        mesh=mesh,
        in_specs=placed,
        out_specs=(P(("row", "col"), None), P(("row", "col"), None)),
        check_vma=False,
    )
```

```python
import functools

import jax
import jax.numpy as jnp
from jax import lax
from jax.experimental import pallas as pl
from jax.experimental.pallas import tpu as pltpu
from jax.sharding import PartitionSpec as P

MESH = pl.DeviceIdType.MESH
PAD, OWN, QUAD, LANES = 16, 12, 4, 128
F32 = jnp.float32
BF16 = jnp.bfloat16


def spots(main):
    return [
        (QUAD * q, LANES * h, LANES * (3 * h + q)) for h in range(2) for q in range(3)
    ]


def partner(me, step, count):
    if count & (count - 1):
        return lax.rem(me + step, count), lax.rem(me + count - step, count)
    bit = 1
    peer = me
    while bit <= step:
        if step & bit:
            peer = peer + bit * (1 - 2 * lax.rem(me // bit, 2))
        bit *= 2
    return peer, peer


def unit_rows(values):
    scale = lax.rsqrt(jnp.sum(values * values, axis=1, keepdims=True) + 1e-06)
    return values * scale, scale


def back_through(unit, scale, upstream):
    inner = jnp.sum(unit * upstream, axis=1, keepdims=True)
    return scale * (upstream - unit * inner)


def kernel(
    n_row, n_col,
    mul_ref, off_ref, ids_hbm, img_hbm, txt_hbm, img_grad, txt_grad,
    ids_ref, img_raw, txt_raw, img_unit, txt_unit,
    img_all, txt_all, img_tail, txt_tail, img_sum, txt_sum, img_part, txt_part, img_in, txt_in,
    load_sem, img_send, img_recv, txt_send, txt_recv, img_back, img_got, txt_back, txt_got,
):
    row, col = lax.axis_index("row"), lax.axis_index("col")
    loads = [
        pltpu.make_async_copy(txt_hbm, txt_raw, load_sem.at[0]),
        pltpu.make_async_copy(img_hbm, img_raw, load_sem.at[1]),
        pltpu.make_async_copy(ids_hbm, ids_ref, load_sem.at[2]),
    ]
    for load in loads:
        load.start()

    col_peer = [None] + [partner(col, d, n_col) for d in range(1, n_col)]
    row_peer = [None] + [partner(row, d, n_row) for d in range(1, n_row)]
    barrier = pltpu.get_barrier_semaphore()
    for d in range(1, n_col):
        pl.semaphore_signal(barrier, inc=1, device_id=(row, col_peer[d][1]), device_id_type=MESH)
    for d in range(1, n_row):
        pl.semaphore_signal(barrier, inc=1, device_id=(row_peer[d][1], col), device_id_type=MESH)

    width = img_raw.shape[1]
    main = img_all.shape[1]
    rest = width - main
    places = spots(main)

    place = lax.broadcasted_iota(jnp.int32, (n_col * PAD, 1), 0)
    slot, entry = place // PAD, lax.rem(place, PAD)
    owner = jnp.zeros((n_col * PAD, 1), jnp.int32) + col
    for d in range(1, n_col):
        owner = jnp.where(slot == d, col_peer[d][1], owner)
    img_ids = (row * n_col + owner) * OWN + entry
    at = lax.broadcasted_iota(jnp.int32, (1, n_row * PAD), 1)
    real = (entry < OWN) & (lax.rem(at, PAD) < OWN)
    zeros = jnp.zeros((PAD - OWN, rest), F32)
    for tail, count in ((img_tail, n_col), (txt_tail, n_row)):
        for d in range(count):
            tail[pl.ds(d * PAD + OWN, PAD - OWN)] = zeros

    loads[2].wait()
    lane = lax.rem(lax.broadcasted_iota(jnp.int32, (1, LANES), 1), PAD)
    numbers = jnp.zeros((1, LANES), jnp.int32)
    for t in range(OWN):
        numbers = jnp.where(lane == t, ids_ref[t], numbers)
    low = lax.rem(numbers, 256).astype(F32)
    high = (numbers // 256).astype(F32)

    free = pl.ds(main - LANES, LANES)
    img_sum[pl.ds(OWN, QUAD), free] = jnp.zeros((QUAD, LANES), F32)
    txt_sum[pl.ds(OWN, QUAD), free] = jnp.concatenate([low, high, low, high], axis=0)

    def pack(raw, unit, tail, packed, whole):
        value, scale = unit_rows(raw[...].astype(F32))
        unit[...] = value
        tail[pl.ds(0, OWN)] = value[:, main:]
        packed[pl.ds(0, OWN)] = value[:, :main]
        for first, lanes, to in places:
            packed[pl.ds(OWN, QUAD), pl.ds(to, LANES)] = value[
                first : first + QUAD, main + lanes : main + lanes + LANES
            ]
        whole[pl.ds(0, PAD)] = packed[pl.ds(0, PAD)].astype(BF16)
        return scale

    def send(src, dst, d, sems, peer):
        return pltpu.make_async_remote_copy(
            src_ref=src, dst_ref=dst.at[pl.ds(d * PAD, PAD)],
            send_sem=sems[0].at[d], recv_sem=sems[1].at[d],
            device_id=peer, device_id_type=MESH,
        )

    txt_copies = [
        send(txt_all.at[pl.ds(0, PAD)], txt_all, d, (txt_send, txt_recv), (row_peer[d][0], col))
        for d in range(1, n_row)
    ]
    img_copies = [
        send(img_all.at[pl.ds(0, PAD)], img_all, d, (img_send, img_recv), (row, col_peer[d][0]))
        for d in range(1, n_col)
    ]
    loads[0].wait()
    txt_scale = pack(txt_raw, txt_unit, txt_tail, txt_sum, txt_all)
    pl.semaphore_wait(barrier, n_col + n_row - 2)
    for copy in reversed(txt_copies):
        copy.start()
    loads[1].wait()
    img_scale = pack(img_raw, img_unit, img_tail, img_sum, img_all)
    for copy in reversed(img_copies):
        copy.start()

    def unpack(whole, tail, d):
        block = whole[pl.ds(d * PAD, PAD), pl.ds(0, main - LANES)].astype(F32)
        for first, lanes, to in places:
            tail[pl.ds(d * PAD + first, QUAD), pl.ds(lanes, LANES)] = block[
                OWN:, to : to + LANES
            ]

    for d, copy in enumerate(img_copies, 1):
        copy.wait_recv()
        unpack(img_all, img_tail, d)
    for d, copy in enumerate(txt_copies, 1):
        copy.wait_recv()
        unpack(txt_all, txt_tail, d)
    digits = []
    for digit in range(2):
        line = jnp.zeros((1, n_row * PAD), F32)
        for d in range(n_row):
            block = txt_all[pl.ds(d * PAD, PAD), free].astype(F32)[OWN + digit : OWN + digit + 1]
            if n_row * PAD > LANES:
                block = jnp.concatenate([block] * (n_row * PAD // LANES), axis=1)
            line = jnp.where(at // PAD == d, block[:, : n_row * PAD], line)
        digits.append(line)
    txt_ids = (digits[0] + 256.0 * digits[1]).astype(jnp.int32)
    texts, text_tails = txt_all[...], txt_tail[...].astype(BF16)
    multiplier, offset = mul_ref[...], off_ref[...]
    across = (((1,), (1,)), ((), ()))
    down = (((0,), (0,)), ((), ()))

    def weigh(first, count):
        rows = pl.ds(first * PAD, count * PAD)
        logits = multiplier * (
            lax.dot_general(img_all[rows], texts, across, preferred_element_type=F32)
            + lax.dot_general(
                img_tail[rows].astype(BF16), text_tails, across, preferred_element_type=F32
            )
        ) + offset
        span = slice(first * PAD, (first + count) * PAD)
        match = img_ids[span] == txt_ids
        weights = jnp.where(match, -multiplier, multiplier) * jax.nn.sigmoid(
            jnp.where(match, -logits, logits)
        )
        return jnp.where(real[span], weights, 0.0).astype(BF16)

    def partial(head, tail, total, part, copies, start, count):
        total[pl.ds(start * PAD, count * PAD)] = head
        for d in reversed(range(count)):
            for first, lanes, to in places:
                total[pl.ds((start + d) * PAD + OWN, QUAD), pl.ds(to, LANES)] = tail[
                    d * PAD + first : d * PAD + first + QUAD, lanes : lanes + LANES
                ]
            if start + d:
                block = pl.ds((start + d) * PAD, PAD)
                part[block] = total[block].astype(BF16)
                copies[start + d - 1].start()

    img_backs = [
        send(img_part.at[pl.ds(d * PAD, PAD)], img_in, d, (img_back, img_got), (row, col_peer[d][1]))
        for d in range(1, n_col)
    ]
    txt_backs = [
        send(txt_part.at[pl.ds(d * PAD, PAD)], txt_in, d, (txt_back, txt_got), (row_peer[d][1], col))
        for d in range(1, n_row)
    ]

    def img_partial(weights, first, count):
        partial(
            jnp.dot(weights, texts, preferred_element_type=F32),
            jnp.dot(weights, text_tails, preferred_element_type=F32),
            img_sum, img_part, img_backs, first, count,
        )

    weights = weigh(0, n_col)
    partial(
        lax.dot_general(weights, img_all[...], down, preferred_element_type=F32),
        lax.dot_general(weights, img_tail[...].astype(BF16), down, preferred_element_type=F32),
        txt_sum, txt_part, txt_backs, 0, n_row,
    )
    img_partial(weights, 0, n_col)

    def finish(grad, total, copies, arrived, unit, scale):
        up = total[pl.ds(0, PAD)]
        for d, copy in enumerate(copies, 1):
            copy.wait_recv()
            up = up + arrived[pl.ds(d * PAD, PAD)].astype(F32)
        grad[:, pl.ds(0, main)] = up[:OWN]
        for first, lanes, to in places:
            grad[pl.ds(first, QUAD), pl.ds(main + lanes, LANES)] = up[OWN:, to : to + LANES]
        grad[...] = back_through(unit[...], scale, grad[...])

    finish(img_grad, img_sum, img_backs, img_in, img_unit, img_scale)
    finish(txt_grad, txt_sum, txt_backs, txt_in, txt_unit, txt_scale)
    for copy in txt_copies + img_copies + img_backs + txt_backs:
        copy.wait_send()


def store(img_ref, txt_ref, img_out, txt_out, sem):
    copies = [
        pltpu.make_async_copy(img_ref, img_out, sem.at[0]),
        pltpu.make_async_copy(txt_ref, txt_out, sem.at[1]),
    ]
    for copy in copies:
        copy.start()
    for copy in copies:
        copy.wait()


def solution(mesh):
    n_row, n_col = mesh.shape["row"], mesh.shape["col"]
    placed = (P(("row", "col"), None), P(("row", "col"), None), P(("row", "col")), P(), P())

    def shards(photo_features, sentence_features, described_photo_number, multiplier, offset):
        own, width = photo_features.shape
        assert own == OWN and width % LANES == 0
        main = width - 2 * LANES
        assert main == 7 * LANES
        smem = pl.BlockSpec(memory_space=pltpu.SMEM)
        hbm = pl.BlockSpec(memory_space=pltpu.HBM)
        vmem = pl.BlockSpec(memory_space=pltpu.VMEM)
        held = pltpu.VMEM((own, width), F32)
        dma = pltpu.SemaphoreType.DMA
        rows, cols = n_row * PAD, n_col * PAD
        grads = pl.pallas_call(
            functools.partial(kernel, n_row, n_col),
            out_shape=(held, held),
            in_specs=[smem, smem, hbm, hbm, hbm],
            out_specs=(vmem, vmem),
            scratch_shapes=[
                pltpu.SMEM((own,), jnp.int32),
                pltpu.VMEM((own, width), BF16),
                pltpu.VMEM((own, width), BF16),
                pltpu.VMEM((own, width), F32),
                pltpu.VMEM((own, width), F32),
                pltpu.VMEM((cols, main), BF16),
                pltpu.VMEM((rows, main), BF16),
                pltpu.VMEM((cols, width - main), F32),
                pltpu.VMEM((rows, width - main), F32),
                pltpu.VMEM((cols, main), F32),
                pltpu.VMEM((rows, main), F32),
                pltpu.VMEM((cols, main), BF16),
                pltpu.VMEM((rows, main), BF16),
                pltpu.VMEM((cols, main), BF16),
                pltpu.VMEM((rows, main), BF16),
                dma((3,)),
                dma((n_col,)), dma((n_col,)), dma((n_row,)), dma((n_row,)),
                dma((n_col,)), dma((n_col,)), dma((n_row,)), dma((n_row,)),
            ],
            compiler_params=pltpu.CompilerParams(
                collective_id=0, has_side_effects=True, vmem_limit_bytes=60 * 2**20
            ),
        )(multiplier, offset, described_photo_number, photo_features, sentence_features)
        grad = jax.ShapeDtypeStruct((own, width), F32)
        return pl.pallas_call(
            store,
            out_shape=(grad, grad),
            in_specs=[vmem, vmem],
            out_specs=(hbm, hbm),
            scratch_shapes=[dma((2,))],
            compiler_params=pltpu.CompilerParams(vmem_limit_bytes=2**20),
        )(*grads)

    return jax.shard_map(
        shards,
        mesh=mesh,
        in_specs=placed,
        out_specs=(P(("row", "col"), None), P(("row", "col"), None)),
        check_vma=False,
    )
```

```python
import functools

import jax
import jax.numpy as jnp
from jax import lax
from jax.experimental import pallas as pl
from jax.experimental.pallas import tpu as pltpu
from jax.sharding import PartitionSpec as P

MESH = pl.DeviceIdType.MESH
PAD, OWN, QUAD, LANES = 16, 12, 4, 128
F32 = jnp.float32
BF16 = jnp.bfloat16


def spots(main):
    return [
        (QUAD * q, LANES * h, LANES * (3 * h + q)) for h in range(2) for q in range(3)
    ]


def partner(me, step, count):
    if count & (count - 1):
        return lax.rem(me + step, count), lax.rem(me + count - step, count)
    bit = 1
    peer = me
    while bit <= step:
        if step & bit:
            peer = peer + bit * (1 - 2 * lax.rem(me // bit, 2))
        bit *= 2
    return peer, peer


def unit_rows(values):
    scale = lax.rsqrt(jnp.sum(values * values, axis=1, keepdims=True) + 1e-06)
    return values * scale, scale


def back_through(unit, scale, upstream):
    inner = jnp.sum(unit * upstream, axis=1, keepdims=True)
    return scale * (upstream - unit * inner)


def kernel(
    n_row, n_col,
    mul_ref, off_ref, ids_hbm, img_hbm, txt_hbm, img_grad, txt_grad,
    ids_ref, img_raw, txt_raw, img_unit, txt_unit,
    img_all, txt_all, img_tail, txt_tail, img_sum, txt_sum, img_part, txt_part, img_in, txt_in,
    load_sem, img_send, img_recv, txt_send, txt_recv, img_back, img_got, txt_back, txt_got,
):
    row, col = lax.axis_index("row"), lax.axis_index("col")
    loads = [
        pltpu.make_async_copy(txt_hbm, txt_raw, load_sem.at[0]),
        pltpu.make_async_copy(img_hbm, img_raw, load_sem.at[1]),
        pltpu.make_async_copy(ids_hbm, ids_ref, load_sem.at[2]),
    ]
    for load in loads:
        load.start()

    col_peer = [None] + [partner(col, d, n_col) for d in range(1, n_col)]
    row_peer = [None] + [partner(row, d, n_row) for d in range(1, n_row)]
    barrier = pltpu.get_barrier_semaphore()
    for d in range(1, n_col):
        pl.semaphore_signal(barrier, inc=1, device_id=(row, col_peer[d][1]), device_id_type=MESH)
    for d in range(1, n_row):
        pl.semaphore_signal(barrier, inc=1, device_id=(row_peer[d][1], col), device_id_type=MESH)

    width = img_raw.shape[1]
    main = img_all.shape[1]
    rest = width - main
    places = spots(main)

    place = lax.broadcasted_iota(jnp.int32, (n_col * PAD, 1), 0)
    slot, entry = place // PAD, lax.rem(place, PAD)
    owner = jnp.zeros((n_col * PAD, 1), jnp.int32) + col
    for d in range(1, n_col):
        owner = jnp.where(slot == d, col_peer[d][1], owner)
    img_ids = (row * n_col + owner) * OWN + entry
    at = lax.broadcasted_iota(jnp.int32, (1, n_row * PAD), 1)
    real = (entry < OWN) & (lax.rem(at, PAD) < OWN)
    zeros = jnp.zeros((PAD - OWN, rest), F32)
    for tail, count in ((img_tail, n_col), (txt_tail, n_row)):
        for d in range(count):
            tail[pl.ds(d * PAD + OWN, PAD - OWN)] = zeros

    loads[2].wait()
    lane = lax.rem(lax.broadcasted_iota(jnp.int32, (1, LANES), 1), PAD)
    numbers = jnp.zeros((1, LANES), jnp.int32)
    for t in range(OWN):
        numbers = jnp.where(lane == t, ids_ref[t], numbers)
    low = lax.rem(numbers, 256).astype(F32)
    high = (numbers // 256).astype(F32)

    def pack(raw, unit, whole, tail, packed):
        value, scale = unit_rows(raw[...].astype(F32))
        unit[...] = value
        tail[pl.ds(0, OWN)] = value[:, main:]
        packed[pl.ds(0, OWN)] = value[:, :main]
        for first, lanes, to in places:
            packed[pl.ds(OWN, QUAD), pl.ds(to, LANES)] = tail[
                pl.ds(first, QUAD), pl.ds(lanes, LANES)
            ]
        return scale

    free = pl.ds(main - LANES, LANES)
    loads[0].wait()
    txt_pack = txt_sum.at[pl.ds(0, PAD)]
    txt_scale = pack(txt_raw, txt_unit, txt_all, txt_tail, txt_pack)
    txt_pack[pl.ds(OWN, QUAD), free] = jnp.zeros((QUAD, LANES), F32)
    txt_pack[pl.ds(OWN, 1), free] = low
    txt_pack[pl.ds(OWN + 1, 1), free] = high
    txt_all[pl.ds(0, PAD)] = txt_pack[...].astype(BF16)
    loads[1].wait()
    img_pack = img_sum.at[pl.ds(0, PAD)]
    img_scale = pack(img_raw, img_unit, img_all, img_tail, img_pack)
    img_pack[pl.ds(OWN, QUAD), free] = jnp.zeros((QUAD, LANES), F32)
    img_all[pl.ds(0, PAD)] = img_pack[...].astype(BF16)

    pl.semaphore_wait(barrier, n_col + n_row - 2)

    def send(src, dst, d, sems, peer):
        return pltpu.make_async_remote_copy(
            src_ref=src, dst_ref=dst.at[pl.ds(d * PAD, PAD)],
            send_sem=sems[0].at[d], recv_sem=sems[1].at[d],
            device_id=peer, device_id_type=MESH,
        )

    txt_copies = [
        send(txt_all.at[pl.ds(0, PAD)], txt_all, d, (txt_send, txt_recv), (row_peer[d][0], col))
        for d in range(1, n_row)
    ]
    img_copies = [
        send(img_all.at[pl.ds(0, PAD)], img_all, d, (img_send, img_recv), (row, col_peer[d][0]))
        for d in range(1, n_col)
    ]
    for copy in reversed(txt_copies):
        copy.start()
    for copy in reversed(img_copies):
        copy.start()

    def unpack(whole, tail, d):
        block = whole[pl.ds(d * PAD, PAD), pl.ds(0, main - LANES)].astype(F32)
        for first, lanes, to in places:
            tail[pl.ds(d * PAD + first, QUAD), pl.ds(lanes, LANES)] = block[
                OWN:, to : to + LANES
            ]

    img_copies[0].wait_recv()
    unpack(img_all, img_tail, 1)
    for d, copy in enumerate(txt_copies, 1):
        copy.wait_recv()
        unpack(txt_all, txt_tail, d)
    digits = []
    for digit in range(2):
        line = jnp.zeros((1, n_row * PAD), F32)
        for d in range(n_row):
            block = txt_all[pl.ds(d * PAD, PAD), free].astype(F32)[OWN + digit : OWN + digit + 1]
            if n_row * PAD > LANES:
                block = jnp.concatenate([block] * (n_row * PAD // LANES), axis=1)
            line = jnp.where(at // PAD == d, block[:, : n_row * PAD], line)
        digits.append(line)
    txt_ids = (digits[0] + 256.0 * digits[1]).astype(jnp.int32)
    texts, text_tails = txt_all[...], txt_tail[...].astype(BF16)
    multiplier, offset = mul_ref[...], off_ref[...]
    for d, copy in enumerate(img_copies[1:], 2):
        copy.wait_recv()
        unpack(img_all, img_tail, d)

    photos, photo_tails = img_all[...], img_tail[...].astype(BF16)
    across = (((1,), (1,)), ((), ()))
    logits = multiplier * (
        lax.dot_general(photos, texts, across, preferred_element_type=F32)
        + lax.dot_general(photo_tails, text_tails, across, preferred_element_type=F32)
    ) + offset
    match = img_ids == txt_ids
    weights = jnp.where(match, -multiplier, multiplier) * jax.nn.sigmoid(
        jnp.where(match, -logits, logits)
    )
    weights = jnp.where(real, weights, 0.0).astype(BF16)

    def partial(head, tail, total, part, copies, count):
        total[...] = head
        for d in reversed(range(count)):
            for first, lanes, to in places:
                total[pl.ds(d * PAD + OWN, QUAD), pl.ds(to, LANES)] = tail[
                    d * PAD + first : d * PAD + first + QUAD, lanes : lanes + LANES
                ]
            if d:
                block = pl.ds(d * PAD, PAD)
                part[block] = total[block].astype(BF16)
                copies[d - 1].start()

    img_backs = [
        send(img_part.at[pl.ds(d * PAD, PAD)], img_in, d, (img_back, img_got), (row, col_peer[d][1]))
        for d in range(1, n_col)
    ]
    partial(
        jnp.dot(weights, texts, preferred_element_type=F32),
        jnp.dot(weights, text_tails, preferred_element_type=F32),
        img_sum, img_part, img_backs, n_col,
    )
    txt_backs = [
        send(txt_part.at[pl.ds(d * PAD, PAD)], txt_in, d, (txt_back, txt_got), (row_peer[d][1], col))
        for d in range(1, n_row)
    ]
    down = (((0,), (0,)), ((), ()))
    partial(
        lax.dot_general(weights, photos, down, preferred_element_type=F32),
        lax.dot_general(weights, photo_tails, down, preferred_element_type=F32),
        txt_sum, txt_part, txt_backs, n_row,
    )

    def finish(grad, total, copies, arrived, unit, scale):
        up = total[pl.ds(0, PAD)]
        for d, copy in enumerate(copies, 1):
            copy.wait_recv()
            up = up + arrived[pl.ds(d * PAD, PAD)].astype(F32)
        grad[:, pl.ds(0, main)] = up[:OWN]
        for first, lanes, to in places:
            grad[pl.ds(first, QUAD), pl.ds(main + lanes, LANES)] = up[OWN:, to : to + LANES]
        grad[...] = back_through(unit[...], scale, grad[...])

    finish(img_grad, img_sum, img_backs, img_in, img_unit, img_scale)
    finish(txt_grad, txt_sum, txt_backs, txt_in, txt_unit, txt_scale)
    for copy in txt_copies + img_copies + img_backs + txt_backs:
        copy.wait_send()


def store(img_ref, txt_ref, img_out, txt_out, sem):
    copies = [
        pltpu.make_async_copy(img_ref, img_out, sem.at[0]),
        pltpu.make_async_copy(txt_ref, txt_out, sem.at[1]),
    ]
    for copy in copies:
        copy.start()
    for copy in copies:
        copy.wait()


def solution(mesh):
    n_row, n_col = mesh.shape["row"], mesh.shape["col"]
    placed = (P(("row", "col"), None), P(("row", "col"), None), P(("row", "col")), P(), P())

    def shards(photo_features, sentence_features, described_photo_number, multiplier, offset):
        own, width = photo_features.shape
        assert own == OWN and width % LANES == 0
        main = width - 2 * LANES
        assert main == 7 * LANES
        smem = pl.BlockSpec(memory_space=pltpu.SMEM)
        hbm = pl.BlockSpec(memory_space=pltpu.HBM)
        vmem = pl.BlockSpec(memory_space=pltpu.VMEM)
        held = pltpu.VMEM((own, width), F32)
        dma = pltpu.SemaphoreType.DMA
        rows, cols = n_row * PAD, n_col * PAD
        grads = pl.pallas_call(
            functools.partial(kernel, n_row, n_col),
            out_shape=(held, held),
            in_specs=[smem, smem, hbm, hbm, hbm],
            out_specs=(vmem, vmem),
            scratch_shapes=[
                pltpu.SMEM((own,), jnp.int32),
                pltpu.VMEM((own, width), BF16),
                pltpu.VMEM((own, width), BF16),
                pltpu.VMEM((own, width), F32),
                pltpu.VMEM((own, width), F32),
                pltpu.VMEM((cols, main), BF16),
                pltpu.VMEM((rows, main), BF16),
                pltpu.VMEM((cols, width - main), F32),
                pltpu.VMEM((rows, width - main), F32),
                pltpu.VMEM((cols, main), F32),
                pltpu.VMEM((rows, main), F32),
                pltpu.VMEM((cols, main), BF16),
                pltpu.VMEM((rows, main), BF16),
                pltpu.VMEM((cols, main), BF16),
                pltpu.VMEM((rows, main), BF16),
                dma((3,)),
                dma((n_col,)), dma((n_col,)), dma((n_row,)), dma((n_row,)),
                dma((n_col,)), dma((n_col,)), dma((n_row,)), dma((n_row,)),
            ],
            compiler_params=pltpu.CompilerParams(
                collective_id=0, has_side_effects=True, vmem_limit_bytes=60 * 2**20
            ),
        )(multiplier, offset, described_photo_number, photo_features, sentence_features)
        grad = jax.ShapeDtypeStruct((own, width), F32)
        return pl.pallas_call(
            store,
            out_shape=(grad, grad),
            in_specs=[vmem, vmem],
            out_specs=(hbm, hbm),
            scratch_shapes=[dma((2,))],
            compiler_params=pltpu.CompilerParams(vmem_limit_bytes=2**20),
        )(*grads)

    return jax.shard_map(
        shards,
        mesh=mesh,
        in_specs=placed,
        out_specs=(P(("row", "col"), None), P(("row", "col"), None)),
        check_vma=False,
    )
```
